32 devices in a mesh: req: 16 (over z, y, x), tp: 2 (over core).
Axes of the slice: x: 2, y: 2, z: 4, core: 2. Of those that a mesh axis runs over, the one named last changes fastest.
Arguments:
- tokens: bfloat16 [8192, 2048], P('req', 'tp'), may hold values from -6 to 6
- attn_gain: float32 [2048], replicated, may hold values from 0.1 to 1.9
- w_query: bfloat16 [2048, 1024], P(None, 'tp'), may hold values from -0.25 to 0.25
- key_weight: bfloat16 [2048, 256], P(None, 'tp'), may hold values from -0.125 to 0.125
- value_weight: bfloat16 [2048, 256], P(None, 'tp'), may hold values from -0.125 to 0.125
- w_attn_out: bfloat16 [1024, 2048], P('tp'), may hold values from -1 to 1
- kv_pages: bfloat16 [512, 2, 2, 128, 128], P('req', None, 'tp'), may hold values from -240 to 240
- page_table: int32 [16, 32], P('req'), may hold values from 0 to 511, as said below
- cached_len: int32 [16], P('req'), may hold values from 3072 to 4096, as said below
- w_gate_z: bfloat16 [2048, 1536], P(None, 'tp'), may hold values from -0.125 to 0.125
- w_ssm_in: bfloat16 [2048, 1536], P(None, 'tp'), may hold values from -0.125 to 0.125
- w_bc: bfloat16 [2048, 512], replicated, may hold values from -0.125 to 0.125
- w_dt: bfloat16 [2048, 24], P(None, 'tp'), may hold values from -0.125 to 0.125
- conv_w_x: float32 [4, 1536], P(None, 'tp'), may hold values from -3 to 3
- conv_w_bc: float32 [4, 512], replicated, may hold values from -3 to 3
- conv_x_state: bfloat16 [16, 3, 1536], P('req', None, 'tp'), may hold values from -6 to 6
- conv_bc_state: bfloat16 [16, 3, 512], P('req'), may hold values from -6 to 6
- dt_bias: float32 [24], P('tp'), may hold values from -3 to 0
- decay_rate: float32 [24], P('tp'), may hold values from 0.002 to 0.2
- skip_gain: float32 [24], P('tp'), may hold values from 0.5 to 1.5
- mixer_gain: float32 [1536], P('tp'), may hold values from 0.1 to 1.9
- w_mixer_out: bfloat16 [1536, 2048], P('tp'), may hold values from -0.15625 to 0.15625
- ssm_state: float32 [16, 24, 64, 256], P('req', 'tp'), may hold values from -6 to 6
Outputs:
- mixed: bfloat16 [8192, 2048], P('req', 'tp')
- final_state: float32 [16, 24, 64, 256], P('req', 'tp')
The draws below stay inside these ranges and needn't reach their ends.
Inputs may be any that keep to these rules, and one draw needn't show every extreme that they name: `page_table`: entries are page numbers below 512. Of one request's 32 entries at most 2 lie among the pages of one index of req, and some request has exactly 2 there. Requests in aligned runs of 4 may share their leading entries. `cached_len`: some request has exactly 4096.
All inputs are finite; a program needn't handle non-finite values.
Results may differ from the reference program's by a relative error of at most 0.018.
The reference program's roundings to bfloat16 on the way count: a program that leaves them out, or rounds other values in their place, can miss the bound.
Values may be sent and summed in bfloat16 or wider, within the bound.
No kernel may reach another device: no remote copies, remote signals or barrier semaphores. Data moves between devices by JAX's collectives and lax.ppermute only.
A program may use at most 128 MiB of HBM per device.

```python
import math
import jax
import jax.numpy as jnp
from jax import lax

MODEL_WIDTH = 2048
QUERY_HEADS = 8
KEY_VALUE_HEADS = 2
HEAD_SIZE = 128
MH = 24
MP = 64
MN = 256
KCONV = 4
PAGE_TOKENS = 128
TABLE_ENTRIES = 32
GROUP = 4
NEW_TOKENS = 512
REQS = 16
TOKENS = 8192
PAGES_DEV = 32
PAGE_TOTAL = 512
MAXCTX = 4096
DSSM = 1536


def draw_lengths(key):
    spread = jax.random.randint(jax.random.fold_in(key, 11), (REQS,), 3 * MAXCTX // 4, MAXCTX + 1)
    chosen = jax.random.randint(jax.random.fold_in(key, 12), (), 0, REQS)
    return jnp.where(jnp.arange(REQS) == chosen, MAXCTX, spread).astype(jnp.int32)


def draw_cached_len(key, part):
    return draw_lengths(key)


def draw_page_table(key, part):
    lengths = draw_lengths(key)
    groups = REQS // GROUP
    capacity = PAGES_DEV // REQS
    full_pages = (lengths // PAGE_TOKENS).reshape(groups, GROUP)
    share_top = jnp.minimum(jnp.min(full_pages, axis=1), TABLE_ENTRIES - 1)
    shared = jax.random.randint(jax.random.fold_in(key, 13), (groups,), 0, share_top + 1)
    group_keys = jax.random.split(jax.random.fold_in(key, 14), groups)
    orders = jax.vmap(lambda group_key: jax.random.permutation(group_key, REQS))(group_keys).astype(jnp.int32)
    last_place = (TABLE_ENTRIES - 1) // capacity
    order_index = jnp.arange(REQS, dtype=jnp.int32)
    last_order = orders[groups - 1]
    swapped = jnp.where(last_order == REQS - 1, last_order[last_place], jnp.where(order_index == last_place, REQS - 1, last_order))
    orders = orders.at[groups - 1].set(swapped.astype(jnp.int32))
    request = jnp.arange(REQS, dtype=jnp.int32)
    page_index = jnp.arange(TABLE_ENTRIES, dtype=jnp.int32)
    group_of = request // GROUP
    owners = orders[group_of][:, page_index // capacity]
    leader = group_of * GROUP
    holder = jnp.where(page_index[None, :] < shared[group_of][:, None], leader[:, None], request[:, None])
    slot_ids = holder * capacity + page_index[None, :] % capacity
    return (owners * PAGES_DEV + slot_ids).astype(jnp.int32)


def draw_kv_pages(key, part):
    value_vectors = jnp.clip(jax.random.normal(key, (PAGE_TOTAL, 2, KEY_VALUE_HEADS, PAGE_TOKENS, HEAD_SIZE), jnp.float32), -6.0, 6.0)
    return value_vectors.astype(jnp.bfloat16)


def level_of(key, dims, cuts, smallest, top_value):
    gain, own = 1.0, jax.random.fold_in(key, 6)
    for position, parts in cuts:
        draws = jnp.exp(jax.random.uniform(jax.random.fold_in(own, position), (parts,), jnp.float32, smallest / len(cuts), top_value / len(cuts)))
        gain = gain * jnp.repeat(draws, dims[position] // parts).reshape([-1 if axis == position else 1 for axis in range(len(dims))])
    return gain


def scatter_about(key, extent, scale, limit, cuts=(), kind=jnp.bfloat16):
    values = scale * jax.random.normal(key, extent, jnp.float32)
    if cuts:
        values = values * level_of(key, extent, cuts, -0.22, 0.18)
    return jnp.clip(values, -limit, limit).astype(kind)


def setup_inputs(seed: int = 0) -> dict:
    arg_keys = jax.random.split(jax.random.key(seed), 24)
    tokens = scatter_about(arg_keys[0], (TOKENS, MODEL_WIDTH), 1.0, 6.0, ((0, 16), (1, 2)))
    attn_gain = jnp.clip(1.0 + 0.18 * jax.random.normal(arg_keys[1], (MODEL_WIDTH,), jnp.float32), 0.1, 1.9)
    w_query = scatter_about(arg_keys[2], (MODEL_WIDTH, QUERY_HEADS * HEAD_SIZE), (MODEL_WIDTH // 4) ** -0.5, 0.25, ((1, 2),))
    key_weight = scatter_about(arg_keys[3], (MODEL_WIDTH, KEY_VALUE_HEADS * HEAD_SIZE), MODEL_WIDTH ** -0.5, 0.125, ((1, 2),))
    value_weight = scatter_about(arg_keys[4], (MODEL_WIDTH, KEY_VALUE_HEADS * HEAD_SIZE), MODEL_WIDTH ** -0.5, 0.125, ((1, 2),))
    w_attn_out = scatter_about(arg_keys[5], (QUERY_HEADS * HEAD_SIZE, MODEL_WIDTH), (HEAD_SIZE // 4) ** -0.5, 1.0, ((0, 2),))
    kv_pages = draw_kv_pages(jax.random.fold_in(arg_keys[23], 71), 0)
    page_table = draw_page_table(jax.random.fold_in(arg_keys[23], 71), 0)
    cached_len = draw_cached_len(jax.random.fold_in(arg_keys[23], 71), 0)
    w_gate_z = scatter_about(arg_keys[9], (MODEL_WIDTH, DSSM), MODEL_WIDTH ** -0.5, 0.125, ((1, 2),))
    w_ssm_in = scatter_about(arg_keys[10], (MODEL_WIDTH, DSSM), MODEL_WIDTH ** -0.5, 0.125, ((1, 2),))
    w_bc = scatter_about(arg_keys[11], (MODEL_WIDTH, 2 * MN), MODEL_WIDTH ** -0.5, 0.125)
    w_dt = scatter_about(arg_keys[12], (MODEL_WIDTH, MH), MODEL_WIDTH ** -0.5, 0.125, ((1, 2),))
    conv_w_x = scatter_about(arg_keys[13], (KCONV, DSSM), KCONV ** -0.5, 3.0, ((1, 2),), jnp.float32)
    conv_w_bc = scatter_about(arg_keys[14], (KCONV, 2 * MN), KCONV ** -0.5, 3.0, (), jnp.float32)
    conv_x_state = scatter_about(arg_keys[15], (REQS, KCONV - 1, DSSM), 1.0, 6.0, ((0, 16), (2, 2)))
    conv_bc_state = scatter_about(arg_keys[16], (REQS, KCONV - 1, 2 * MN), 1.0, 6.0, ((0, 16),))
    dt_bias = jnp.clip(-3.0 + 3.0 * jax.random.uniform(arg_keys[17], (MH,), jnp.float32) ** level_of(arg_keys[17], (MH,), ((0, 2),), -0.2, 0.2), -3.0, 0.0)
    decay_rate = jnp.clip(jnp.exp(math.log(0.2) - 4.6051702 * jax.random.uniform(arg_keys[18], (MH,), jnp.float32) ** level_of(arg_keys[18], (MH,), ((0, 2),), -0.2, 0.2)), 0.002, 0.2)
    skip_gain = jnp.clip(0.5 + 1.0 * jax.random.uniform(arg_keys[19], (MH,), jnp.float32) ** level_of(arg_keys[19], (MH,), ((0, 2),), -0.2, 0.2), 0.5, 1.5)
    mixer_gain = jnp.clip(1.0 + 0.18 * jax.random.normal(arg_keys[20], (DSSM,), jnp.float32), 0.1, 1.9)
    w_mixer_out = scatter_about(arg_keys[21], (DSSM, MODEL_WIDTH), DSSM ** -0.5, 0.15625, ((0, 2),))
    ssm_state = scatter_about(arg_keys[22], (REQS, MH, MP, MN), 1.0, 6.0, ((0, 16), (1, 2)), jnp.float32)
    return dict(tokens=tokens, attn_gain=attn_gain, w_query=w_query, key_weight=key_weight, value_weight=value_weight, w_attn_out=w_attn_out, kv_pages=kv_pages, page_table=page_table, cached_len=cached_len, w_gate_z=w_gate_z, w_ssm_in=w_ssm_in, w_bc=w_bc, w_dt=w_dt, conv_w_x=conv_w_x, conv_w_bc=conv_w_bc, conv_x_state=conv_x_state, conv_bc_state=conv_bc_state, dt_bias=dt_bias, decay_rate=decay_rate, skip_gain=skip_gain, mixer_gain=mixer_gain, w_mixer_out=w_mixer_out, ssm_state=ssm_state)


EPSILON = 1e-05
ROPE_BASE = 100000.0
NEG_FILL = -1e+30

def rms_scale(value_vectors, gain_row):
    mean_sq = lax.optimization_barrier(jnp.mean(value_vectors * value_vectors, axis=-1, keepdims=True))
    return value_vectors * lax.rsqrt(mean_sq + EPSILON) * gain_row

def stored(value_vectors):
    return lax.optimization_barrier(value_vectors.astype(jnp.bfloat16))

def apply_rotary(value_vectors, token_positions):
    full_width = value_vectors.shape[-1]
    half_width = full_width // 2
    inverse = ROPE_BASE ** (-2.0 * jnp.arange(half_width, dtype=jnp.float32) / full_width)
    angles = token_positions.astype(jnp.float32)[:, None] * inverse[None, :]
    cosine = jnp.concatenate([jnp.cos(angles), jnp.cos(angles)], axis=-1)[:, None, :]
    sine_row = jnp.concatenate([jnp.sin(angles), jnp.sin(angles)], axis=-1)[:, None, :]
    turned = jnp.concatenate([-value_vectors[..., half_width:], value_vectors[..., :half_width]], axis=-1)
    return value_vectors * cosine + turned * sine_row

def short_conv(history, fresh_rows, kernel):
    joined = jnp.concatenate([history, fresh_rows], axis=0).astype(jnp.float32)
    row_count = fresh_rows.shape[0]
    summed = joined[0:row_count] * kernel[0]
    for tap_index in range(1, kernel.shape[0]):
        summed = summed + joined[tap_index:tap_index + row_count] * kernel[tap_index]
    return jax.nn.silu(summed)

def ssm_block(ssm_x, step_size, decay_rate, b_vectors, c_vectors, state_in, skip_gain):
    row_count = ssm_x.shape[0]
    row_order = jnp.arange(row_count, dtype=jnp.int32)
    causal = row_order[None, :] <= row_order[:, None]
    cumulative = jnp.cumsum(-step_size * decay_rate, axis=0)
    gap = cumulative.T[:, :, None] - cumulative.T[:, None, :]
    inner = jnp.dot(c_vectors.astype(jnp.float32), b_vectors.astype(jnp.float32).T, precision=lax.Precision.HIGHEST)
    mixing = stored(jnp.where(causal[None], jnp.exp(jnp.minimum(gap, 0.0)), 0.0) * inner[None])
    x_float = ssm_x.astype(jnp.float32)
    moved_float = x_float * step_size[:, :, None]
    moved = stored(moved_float)
    intra = jnp.einsum('hij,jhp->ihp', mixing.astype(jnp.float32), moved.astype(jnp.float32), precision=lax.Precision.HIGHEST)
    carried = jnp.exp(cumulative)[:, :, None] * jnp.einsum('in,hpn->ihp', c_vectors.astype(jnp.float32), state_in, precision=lax.Precision.HIGHEST)
    ssm_y = intra + carried + skip_gain[None, :, None] * x_float
    tail_fade = jnp.exp(cumulative[-1][None, :] - cumulative)
    tail_moved = stored(moved_float * tail_fade[:, :, None])
    last_state = jnp.exp(cumulative[-1])[:, None, None] * state_in + jnp.einsum('jhp,jn->hpn', tail_moved.astype(jnp.float32), b_vectors.astype(jnp.float32), precision=lax.Precision.HIGHEST)
    return (ssm_y, last_state)

def reference(tokens, attn_gain, w_query, key_weight, value_weight, w_attn_out, kv_pages, page_table, cached_len, w_gate_z, w_ssm_in, w_bc, w_dt, conv_w_x, conv_w_bc, conv_x_state, conv_bc_state, dt_bias, decay_rate, skip_gain, mixer_gain, w_mixer_out, ssm_state):
    queries_per_group = QUERY_HEADS // KEY_VALUE_HEADS
    score_scale = 1.0 / math.sqrt(HEAD_SIZE)

    def one_request(inputs):
        request_tokens, table_row, length, history_x, history_bc, state_in = inputs
        normed_input = rms_scale(request_tokens.astype(jnp.float32), attn_gain).astype(jnp.bfloat16)
        token_positions = length + jnp.arange(NEW_TOKENS, dtype=jnp.int32)
        query_vectors = apply_rotary(jnp.dot(normed_input, w_query, preferred_element_type=jnp.float32).reshape(NEW_TOKENS, QUERY_HEADS, HEAD_SIZE), token_positions).astype(jnp.bfloat16)
        incoming_keys = apply_rotary(jnp.dot(normed_input, key_weight, preferred_element_type=jnp.float32).reshape(NEW_TOKENS, KEY_VALUE_HEADS, HEAD_SIZE), token_positions).astype(jnp.bfloat16)
        incoming_values = jnp.dot(normed_input, value_weight, preferred_element_type=jnp.float32).astype(jnp.bfloat16).reshape(NEW_TOKENS, KEY_VALUE_HEADS, HEAD_SIZE)
        page_table_rows = kv_pages[table_row]
        cached_key_rows = jnp.transpose(page_table_rows[:, 0], (1, 0, 2, 3)).reshape(KEY_VALUE_HEADS, TABLE_ENTRIES * PAGE_TOKENS, HEAD_SIZE)
        cached_value_rows = jnp.transpose(page_table_rows[:, 1], (1, 0, 2, 3)).reshape(KEY_VALUE_HEADS, TABLE_ENTRIES * PAGE_TOKENS, HEAD_SIZE)
        all_keys = jnp.concatenate([cached_key_rows, jnp.transpose(incoming_keys, (1, 0, 2))], axis=1).astype(jnp.float32)
        all_vals = jnp.concatenate([cached_value_rows, jnp.transpose(incoming_values, (1, 0, 2))], axis=1).astype(jnp.float32)
        cache_slots = jnp.arange(TABLE_ENTRIES * PAGE_TOKENS, dtype=jnp.int32)
        row_order = jnp.arange(NEW_TOKENS, dtype=jnp.int32)
        visible = jnp.concatenate([jnp.broadcast_to(cache_slots[None, :] < length, (NEW_TOKENS, TABLE_ENTRIES * PAGE_TOKENS)), row_order[None, :] <= row_order[:, None]], axis=1)
        query_groups = query_vectors.reshape(NEW_TOKENS, KEY_VALUE_HEADS, queries_per_group, HEAD_SIZE).astype(jnp.float32)
        scores = jnp.einsum('nhgd,hkd->hgnk', query_groups, all_keys) * score_scale
        scores = jnp.where(visible, scores, NEG_FILL)
        row_top = lax.optimization_barrier(jnp.max(scores, axis=-1, keepdims=True))
        weights = jnp.where(visible, jnp.exp(scores - row_top), 0.0)
        weight_sum = lax.optimization_barrier(jnp.sum(weights, axis=-1, keepdims=True))
        rounded = lax.optimization_barrier(weights.astype(jnp.bfloat16)).astype(jnp.float32)
        context = jnp.einsum('hgnk,hkd->hgnd', rounded, all_vals) / weight_sum
        context = jnp.transpose(context, (2, 0, 1, 3)).reshape(NEW_TOKENS, QUERY_HEADS * HEAD_SIZE).astype(jnp.bfloat16)
        attn_part = jnp.dot(context, w_attn_out, preferred_element_type=jnp.float32)
        gate_z = stored(jnp.dot(normed_input, w_gate_z, preferred_element_type=jnp.float32))
        ssm_in = stored(jnp.dot(normed_input, w_ssm_in, preferred_element_type=jnp.float32))
        bc_in = stored(jnp.dot(normed_input, w_bc, preferred_element_type=jnp.float32))
        step_raw = jnp.dot(normed_input, w_dt, preferred_element_type=jnp.float32)
        ssm_x = stored(short_conv(history_x, ssm_in, conv_w_x))
        bc_rows = stored(short_conv(history_bc, bc_in, conv_w_bc))
        step_size = jax.nn.softplus(step_raw + dt_bias)
        ssm_y, last_state = ssm_block(ssm_x.reshape(NEW_TOKENS, MH, MP), step_size, decay_rate, bc_rows[:, :MN], bc_rows[:, MN:], state_in, skip_gain)
        gated = ssm_y.reshape(NEW_TOKENS, DSSM) * jax.nn.silu(gate_z.astype(jnp.float32))
        normed_y = rms_scale(gated, mixer_gain).astype(jnp.bfloat16)
        ssm_part = jnp.dot(normed_y, w_mixer_out, preferred_element_type=jnp.float32)
        return ((attn_part + ssm_part).astype(jnp.bfloat16), last_state)
    mixed, final_state = lax.map(one_request, (tokens.reshape(REQS, NEW_TOKENS, MODEL_WIDTH), page_table, cached_len, conv_x_state, conv_bc_state, ssm_state))
    return (mixed.reshape(TOKENS, MODEL_WIDTH), final_state)
```

```python
import functools

import jax
import jax.numpy as jnp
from jax import lax
from jax.experimental import pallas as pl
from jax.experimental.pallas import tpu as pltpu
from jax.sharding import PartitionSpec as P

HEAD_SIZE = 128
MP = 64
MN = 256
DSSM = 1536

EPSILON = 1e-05
ROPE_BASE = 100000.0
NEG_FILL = -1e30
LOG2E = 1.4426950408889634
SCORE_SCALE = HEAD_SIZE ** (-0.5) * LOG2E
VMEM_BYTES = 56 * 2**20

VMEM = pl.BlockSpec(memory_space=pltpu.VMEM)
SMEM = pl.BlockSpec(memory_space=pltpu.SMEM)
ANY = pl.BlockSpec(memory_space=pl.ANY)
F32 = jnp.float32
BF16 = jnp.bfloat16


def params(*semantics):
    return pltpu.CompilerParams(
        vmem_limit_bytes=VMEM_BYTES, dimension_semantics=semantics or None
    )


def rope_tables(token_positions):
    half_width = HEAD_SIZE // 2
    inverse = ROPE_BASE ** (-2.0 * jnp.arange(half_width, dtype=F32) / HEAD_SIZE)
    angles = token_positions.astype(F32)[:, None] * inverse[None, :]
    cosine, sine = jnp.cos(angles), jnp.sin(angles)
    return (
        jnp.concatenate([cosine, cosine], axis=-1),
        jnp.concatenate([-sine, sine], axis=-1),
    )


def pick_pages(table_row, devices, pages_dev, capacity):
    owners = table_row // pages_dev
    local_slot = table_row % pages_dev
    page_index = jnp.arange(table_row.shape[0], dtype=jnp.int32)
    earlier = (page_index[None, :] < page_index[:, None]) & (owners[None, :] == owners[:, None])
    ranks = jnp.sum(earlier.astype(jnp.int32), axis=1)
    targets = jnp.arange(devices, dtype=jnp.int32)
    places = jnp.arange(capacity, dtype=jnp.int32)
    chosen = (
        (owners[None, None, :] == targets[:, None, None])
        & (ranks[None, None, :] == places[None, :, None])
    ).astype(jnp.int32)
    return (
        jnp.sum(chosen * local_slot, axis=-1),
        jnp.sum(chosen * page_index, axis=-1),
        jnp.sum(chosen, axis=-1),
    )


def gather_kernel(count, want_ref, pages_ref, out_ref, sems):
    copies = [
        pltpu.make_async_copy(pages_ref.at[want_ref[i]], out_ref.at[i], sems.at[i])
        for i in range(count)
    ]
    for copy in copies:
        copy.start()
    for copy in copies:
        copy.wait()


def gather_pages(want, kv_pages):
    count = want.shape[0]
    return pl.pallas_call(
        functools.partial(gather_kernel, count),
        out_shape=jax.ShapeDtypeStruct((count,) + kv_pages.shape[1:], kv_pages.dtype),
        in_specs=[SMEM, ANY],
        out_specs=ANY,
        scratch_shapes=[pltpu.SemaphoreType.DMA((count,))],
        compiler_params=params(),
        cost_estimate=pl.CostEstimate(flops=0, bytes_accessed=8 * 2**20, transcendentals=0),
        name="gather_pages",
    )(want, kv_pages)


def project_kernel(
    core_ref, mine_ref, other_ref, gain_ref, cos_ref, sin_ref,
    wq_hbm, wk_hbm, wv_hbm, wx_hbm, wbc_hbm, wdt_hbm, wz_hbm,
    q_ref, k_ref, v_ref, x_ref, bc_ref, dt_ref, z_ref,
    normed, wq, wkv, wx, wbc, wdt, wz, sems,
):
    copies = [
        pltpu.make_async_copy(source, target, sems.at[i])
        for i, (source, target) in enumerate(
            (
                (wq_hbm, wq),
                (wk_hbm, wkv.at[:, 0:HEAD_SIZE]),
                (wv_hbm, wkv.at[:, HEAD_SIZE : 2 * HEAD_SIZE]),
                (wbc_hbm, wbc),
                (wdt_hbm, wdt),
                (wx_hbm, wx),
                (wz_hbm, wz),
            )
        )
    ]
    for copy in copies:
        copy.start()
    rows, half = mine_ref.shape
    core = core_ref[0]
    here = pl.ds(pl.multiple_of(core * half, half), half)
    there = pl.ds(pl.multiple_of((1 - core) * half, half), half)
    step = 64

    def norm_rows(i, carry):
        block = pl.ds(pl.multiple_of(i * step, step), step)
        mine = mine_ref[block, :].astype(F32)
        other = other_ref[block, :].astype(F32)
        total = jnp.sum(mine * mine + other * other, axis=-1, keepdims=True)
        scale = lax.rsqrt(total / (2 * half) + EPSILON)
        normed[block, here] = (mine * scale * gain_ref[:, here]).astype(BF16)
        normed[block, there] = (other * scale * gain_ref[:, there]).astype(BF16)
        return carry

    lax.fori_loop(0, rows // step, norm_rows, 0)

    def rope(vectors):
        return vectors * cos_ref[...] + pltpu.roll(vectors, HEAD_SIZE // 2, 1) * sin_ref[...]

    copies[0].wait()
    for tile in range(wq.shape[1] // 256):
        two = jnp.dot(
            normed[...], wq[:, tile * 256 : tile * 256 + 256], preferred_element_type=F32
        )
        for side in range(2):
            head = 2 * tile + side
            q_ref[head * rows : (head + 1) * rows, :] = rope(
                two[:, side * HEAD_SIZE : (side + 1) * HEAD_SIZE]
            ).astype(BF16)
    copies[1].wait()
    copies[2].wait()
    two = jnp.dot(normed[...], wkv[...], preferred_element_type=F32)
    k_ref[...] = rope(two[:, :HEAD_SIZE]).astype(BF16)
    v_ref[...] = two[:, HEAD_SIZE:].astype(BF16)
    for index, weight, target in ((3, wbc, bc_ref), (4, wdt, dt_ref), (5, wx, x_ref), (6, wz, z_ref)):
        copies[index].wait()
        width = weight.shape[1]
        for start in range(0, width, 256):
            stop = min(start + 256, width)
            target[:, start:stop] = jnp.dot(
                normed[...], weight[:, start:stop], preferred_element_type=F32
            ).astype(target.dtype)


def project(core, mine, other, gain, cosine, sine, wq, wk, wv, wx, wbc, wdt, wz):
    rows, half = mine.shape
    width = 2 * half

    def out(shape, dtype=BF16):
        return jax.ShapeDtypeStruct(shape, dtype)

    return pl.pallas_call(
        project_kernel,
        out_shape=(
            out((wq.shape[1] // HEAD_SIZE * rows, HEAD_SIZE)),
            out((rows, wk.shape[1])),
            out((rows, wv.shape[1])),
            out((rows, wx.shape[1])),
            out((rows, wbc.shape[1])),
            out((rows, wdt.shape[1]), F32),
            out((rows, wz.shape[1])),
        ),
        in_specs=[SMEM] + [VMEM] * 5 + [ANY] * 7,
        out_specs=(VMEM,) * 7,
        scratch_shapes=[
            pltpu.VMEM((rows, width), BF16),
            pltpu.VMEM(wq.shape, BF16),
            pltpu.VMEM((width, 2 * HEAD_SIZE), BF16),
            pltpu.VMEM(wx.shape, BF16),
            pltpu.VMEM(wbc.shape, BF16),
            pltpu.VMEM(wdt.shape, BF16),
            pltpu.VMEM(wz.shape, BF16),
            pltpu.SemaphoreType.DMA((7,)),
        ],
        compiler_params=params(),
        cost_estimate=pl.CostEstimate(
            flops=6 * 10**9, bytes_accessed=17 * 2**20, transcendentals=0
        ),
        name="project",
    )(core, mine, other, gain, cosine, sine, wq, wk, wv, wx, wbc, wdt, wz)


def silu(value):
    return value / (1.0 + jnp.exp(-value))


def mixer_kernel(
    x_ref, z_ref, bc_ref, dt_ref, histx_ref, histbc_ref, convx_ref, convbc_ref,
    bias_ref, rate_ref, skip_ref, gain_ref, state_ref,
    gated_ref, square_ref, last_ref,
    padded, inner, cum, cum_t, step_size, b_ref, c_ref,
):
    rows = x_ref.shape[0]
    taps = convx_ref.shape[0]
    heads = dt_ref.shape[1]
    group = 2 * MP
    half = rows // 2

    def conv(history, fresh, kernel):
        width = fresh.shape[1]
        padded[0:8, 0:width] = jnp.zeros((8, width), F32)
        padded[8 - (taps - 1) : 8, 0:width] = history.astype(F32)
        padded[8 : 8 + rows, 0:width] = fresh.astype(F32)
        summed = padded[9 - taps : 9 - taps + rows, 0:width] * kernel[0:1, :]
        for tap in range(1, taps):
            begin = 9 - taps + tap
            summed = summed + padded[begin : begin + rows, 0:width] * kernel[tap : tap + 1, :]
        return silu(summed).astype(BF16)

    for start in range(0, 2 * MN, group):
        part = conv(
            histbc_ref[0, :, start : start + group],
            bc_ref[:, start : start + group],
            convbc_ref[:, start : start + group],
        )
        if start < MN:
            b_ref[:, start : start + group] = part
        else:
            c_ref[:, start - MN : start - MN + group] = part

    raw = dt_ref[...] + bias_ref[...]
    size = jnp.maximum(raw, 0.0) + jnp.log1p(jnp.exp(-jnp.abs(raw)))
    step_size[:, 0:heads] = size
    row_index = lax.broadcasted_iota(jnp.int32, (rows, rows), 0)
    column_index = lax.broadcasted_iota(jnp.int32, (rows, rows), 1)
    causal = column_index <= row_index
    drop = jnp.zeros((rows, 128), F32)
    cum[...] = drop
    cum[:, 0:heads] = -size * (rate_ref[...] * LOG2E)
    cum[...] = jnp.dot(
        causal.astype(F32), cum[...], precision=lax.Precision.HIGHEST, preferred_element_type=F32
    )
    cum_t[...] = cum[...].T
    inner[...] = jnp.where(
        causal,
        lax.dot_general(
            c_ref[...], b_ref[...], (((1,), (1,)), ((), ())), preferred_element_type=F32
        ),
        0.0,
    )
    lane = lax.broadcasted_iota(jnp.int32, (1, group), 1)
    first = lane < MP
    first_rows = lax.broadcasted_iota(jnp.int32, (group, 1), 0) < MP
    squares = jnp.zeros((rows, group), F32)
    for pair in range(heads // 2):
        cols = slice(pair * group, (pair + 1) * group)
        one, two = 2 * pair, 2 * pair + 1
        x_rows = conv(histx_ref[0, :, cols], x_ref[:, cols], convx_ref[:, cols]).astype(F32)
        sizes = jnp.where(first, step_size[:, one : one + 1], step_size[:, two : two + 1])
        fades = jnp.where(first, cum[:, one : one + 1], cum[:, two : two + 1])
        last_fade = fades[rows - 1 : rows, :]
        moved_float = x_rows * sizes
        moved = moved_float.astype(BF16)
        tail_moved = moved_float * jnp.exp2(last_fade - fades)
        state = state_ref[cols, :]
        state_high = state.astype(BF16)
        state_low = (state - state_high.astype(F32)).astype(BF16)
        contract = (((1,), (1,)), ((), ()))
        carried = lax.dot_general(
            c_ref[...], state_high, contract, preferred_element_type=F32
        ) + lax.dot_general(c_ref[...], state_low, contract, preferred_element_type=F32)
        blocks = []
        for begin in (0, half):
            end = begin + half
            sides = []
            for head in (one, two):
                gap = cum[begin:end, head : head + 1] - cum_t[head : head + 1, 0:end]
                mixing = (jnp.exp2(jnp.minimum(gap, 0.0)) * inner[begin:end, 0:end]).astype(BF16)
                sides.append(jnp.dot(mixing, moved[0:end, :], preferred_element_type=F32))
            blocks.append(jnp.where(first, sides[0], sides[1]))
        ssm_y = (
            jnp.concatenate(blocks, axis=0)
            + carried * jnp.exp2(fades)
            + skip_ref[:, cols] * x_rows
        )
        gated = ssm_y * silu(z_ref[:, cols].astype(F32))
        squares = squares + gated * gated
        gated_ref[:, cols] = (gated * gain_ref[:, cols]).astype(BF16)
        added = jnp.dot(tail_moved.T.astype(BF16), b_ref[...], preferred_element_type=F32)
        ends = jnp.exp2(cum_t[one : two + 1, rows - 1 : rows])
        keep = jnp.where(first_rows, ends[0:1, :], ends[1:2, :])
        last_ref[cols, :] = keep * state + added
    square_ref[...] = jnp.sum(squares.T, axis=0, keepdims=True)


def mixer(x, z, bc, dt, histx, histbc, convx, convbc, bias, rate, skip, gain, state):
    rows, width = x.shape
    return pl.pallas_call(
        mixer_kernel,
        out_shape=(
            jax.ShapeDtypeStruct((rows, width), BF16),
            jax.ShapeDtypeStruct((1, rows), F32),
            jax.ShapeDtypeStruct(state.shape, F32),
        ),
        in_specs=[VMEM] * 13,
        out_specs=(VMEM,) * 3,
        scratch_shapes=[
            pltpu.VMEM((rows + 8, 2 * MP), F32),
            pltpu.VMEM((rows, rows), F32),
            pltpu.VMEM((rows, 128), F32),
            pltpu.VMEM((128, rows), F32),
            pltpu.VMEM((rows, 128), F32),
            pltpu.VMEM((rows, MN), BF16),
            pltpu.VMEM((rows, MN), BF16),
        ],
        compiler_params=params(),
        cost_estimate=pl.CostEstimate(
            flops=4 * 10**9, bytes_accessed=8 * 2**20, transcendentals=4 * 10**6
        ),
        name="mixer",
    )(x, z, bc, dt, histx, histbc, convx, convbc, bias, rate, skip, gain, state)


def attend_kernel(
    seen_ref, q_ref, fresh_k_ref, fresh_v_ref, kv_hbm, out_ref, keys, values, sems,
):
    pages, _, page_size, _ = kv_hbm.shape
    block = q_ref.shape[0]
    rows = fresh_k_ref.shape[0]
    chunk = 4 * page_size
    index = pl.program_id(0)
    lane_zero = lax.broadcasted_iota(jnp.int32, (page_size, HEAD_SIZE), 1) == 0

    @pl.when(index == 0)
    def _():
        copies = []
        for page in range(pages):
            place = pl.ds(page * page_size, page_size)
            for which, target in ((0, keys), (1, values)):
                copies.append(
                    pltpu.make_async_copy(
                        kv_hbm.at[page, which],
                        target.at[place, 0:HEAD_SIZE],
                        sems.at[2 * page + which],
                    )
                )
        for copy in copies:
            copy.start()
        token = lax.broadcasted_iota(jnp.int32, (page_size, HEAD_SIZE), 0)
        values[:, HEAD_SIZE:] = jnp.ones((pages * page_size, HEAD_SIZE), BF16)
        for page in range(pages):
            hidden = lane_zero & (token >= seen_ref[page])
            keys[page * page_size : (page + 1) * page_size, HEAD_SIZE:] = jnp.where(
                hidden, NEG_FILL, 0.0
            ).astype(BF16)
        for copy in copies:
            copy.wait()

    query = q_ref[...]
    contract = (((1,), (1,)), ((), ()))
    row = lax.broadcasted_iota(jnp.int32, (block, rows), 0) + lax.rem(index * block, rows)
    column = lax.broadcasted_iota(jnp.int32, (block, rows), 1)
    scores = lax.dot_general(query, fresh_k_ref[...], contract, preferred_element_type=F32)
    scores = jnp.where(column <= row, scores, NEG_FILL)
    top = jnp.max(scores, axis=-1, keepdims=True)
    weights = jnp.exp2((scores - top) * SCORE_SCALE).astype(BF16)
    fresh = jnp.concatenate([fresh_v_ref[...], jnp.ones((rows, HEAD_SIZE), BF16)], axis=1)
    total = jnp.dot(weights, fresh, preferred_element_type=F32)
    one_hot = (lax.broadcasted_iota(jnp.int32, (block, HEAD_SIZE), 1) == 0).astype(BF16)
    wide_query = jnp.concatenate([query, one_hot], axis=1)
    for start in range(0, pages * page_size, chunk):
        span = slice(start, min(start + chunk, pages * page_size))
        scores = lax.dot_general(wide_query, keys[span, :], contract, preferred_element_type=F32)
        new_top = jnp.maximum(top, jnp.max(scores, axis=-1, keepdims=True))
        fade = jnp.exp2((top - new_top) * SCORE_SCALE)
        weights = jnp.exp2((scores - new_top) * SCORE_SCALE).astype(BF16)
        total = total * fade + jnp.dot(weights, values[span, :], preferred_element_type=F32)
        top = new_top
    out_ref[...] = (total[:, :HEAD_SIZE] / total[:, HEAD_SIZE:]).astype(BF16)


def attend(seen, queries, fresh_keys, fresh_values, kv):
    pages, _, page_size, _ = kv.shape
    rows = fresh_keys.shape[0]
    block = rows // 2
    per_head = rows // block
    return pl.pallas_call(
        attend_kernel,
        out_shape=jax.ShapeDtypeStruct((rows, queries.shape[0] // rows * HEAD_SIZE), BF16),
        grid=(queries.shape[0] // block,),
        in_specs=[
            SMEM,
            pl.BlockSpec((block, HEAD_SIZE), lambda i: (i, 0)),
            pl.BlockSpec((rows, HEAD_SIZE), lambda i: (0, 0)),
            pl.BlockSpec((rows, HEAD_SIZE), lambda i: (0, 0)),
            ANY,
        ],
        out_specs=pl.BlockSpec((block, HEAD_SIZE), lambda i: (i % per_head, i // per_head)),
        scratch_shapes=[
            pltpu.VMEM((pages * page_size, 2 * HEAD_SIZE), BF16),
            pltpu.VMEM((pages * page_size, 2 * HEAD_SIZE), BF16),
            pltpu.SemaphoreType.DMA((2 * pages,)),
        ],
        compiler_params=params("arbitrary"),
        cost_estimate=pl.CostEstimate(
            flops=16 * 10**9, bytes_accessed=4 * 2**20, transcendentals=10**7
        ),
        name="attend",
    )(seen, queries, fresh_keys, fresh_values, kv)


def mixer_out_kernel(gated_ref, scale_ref, weight_ref, out_ref):
    out_ref[...] = (
        jnp.dot(gated_ref[...], weight_ref[...], preferred_element_type=F32) * scale_ref[...]
    )


def mixer_out(gated, scale, weight):
    rows, depth = gated.shape
    width = weight.shape[1]
    tile = 256
    return pl.pallas_call(
        mixer_out_kernel,
        out_shape=jax.ShapeDtypeStruct((rows, width), F32),
        grid=(width // tile,),
        in_specs=[
            pl.BlockSpec((rows, depth), lambda i: (0, 0)),
            pl.BlockSpec((rows, 1), lambda i: (0, 0)),
            pl.BlockSpec((depth, tile), lambda i: (0, i)),
        ],
        out_specs=pl.BlockSpec((rows, tile), lambda i: (0, i)),
        compiler_params=params("arbitrary"),
        cost_estimate=pl.CostEstimate(
            flops=2 * rows * depth * width, bytes_accessed=8 * 2**20, transcendentals=0
        ),
        name="mixer_out",
    )(gated, scale, weight)


def attn_out_kernel(core_ref, context_ref, weight_ref, part_ref, out_ref):
    out_ref[...] = (
        jnp.dot(context_ref[...], weight_ref[...], preferred_element_type=F32) + part_ref[...]
    ).astype(out_ref.dtype)


def attn_out(core, context, weight, part, dtype):
    rows, depth = context.shape
    tile = 256
    tiles = weight.shape[1] // 2 // tile
    return pl.pallas_call(
        attn_out_kernel,
        out_shape=jax.ShapeDtypeStruct((rows, weight.shape[1] // 2), dtype),
        grid_spec=pltpu.PrefetchScalarGridSpec(
            num_scalar_prefetch=1,
            grid=(tiles,),
            in_specs=[
                pl.BlockSpec((rows, depth), lambda i, core: (0, 0)),
                pl.BlockSpec((depth, tile), lambda i, core: (0, core[0] * tiles + i)),
                pl.BlockSpec((rows, tile), lambda i, core: (0, core[0] * tiles + i)),
            ],
            out_specs=pl.BlockSpec((rows, tile), lambda i, core: (0, i)),
        ),
        compiler_params=params("arbitrary"),
        cost_estimate=pl.CostEstimate(
            flops=rows * depth * weight.shape[1], bytes_accessed=4 * 2**20, transcendentals=0
        ),
        name="attn_out",
    )(core, context, weight, part)


def shards(
    tokens,
    attn_gain,
    w_query,
    key_weight,
    value_weight,
    w_attn_out,
    kv_pages,
    page_table,
    cached_len,
    w_gate_z,
    w_ssm_in,
    w_bc,
    w_dt,
    conv_w_x,
    conv_w_bc,
    conv_x_state,
    conv_bc_state,
    dt_bias,
    decay_rate,
    skip_gain,
    mixer_gain,
    w_mixer_out,
    ssm_state,
):
    swap = [(0, 1), (1, 0)]
    core = lax.axis_index("tp").astype(jnp.int32).reshape(1)
    row_count = tokens.shape[0]
    devices = lax.axis_size("req")
    pages_dev = kv_pages.shape[0]
    capacity = pages_dev // devices
    page_size = kv_pages.shape[3]
    length = cached_len[0]

    want_slot, page_of, present = pick_pages(page_table[0], devices, pages_dev, capacity)
    requested = lax.all_to_all(want_slot, "req", split_axis=0, concat_axis=0, tiled=True)
    other = lax.ppermute(tokens, "tp", swap)
    fetched = gather_pages(
        requested.reshape(-1), kv_pages.reshape((pages_dev, 2, page_size, HEAD_SIZE))
    )
    arrived = lax.all_to_all(
        fetched.reshape((devices, capacity, 2, page_size, HEAD_SIZE)),
        "req",
        split_axis=0,
        concat_axis=0,
        tiled=True,
    ).reshape((devices * capacity, 2, page_size, HEAD_SIZE))
    seen = (present * jnp.clip(length - page_of * page_size, 0, page_size)).reshape(-1)

    cosine, sine = rope_tables(length + jnp.arange(row_count, dtype=jnp.int32))
    queries, fresh_keys, fresh_values, ssm_in, bc_in, step_raw, gate_z = project(
        core, tokens, other, attn_gain[None, :], cosine, sine,
        w_query, key_weight, value_weight, w_ssm_in, w_bc, w_dt, w_gate_z,
    )
    heads = w_dt.shape[1]
    gated, squares, last_state = mixer(
        ssm_in, gate_z, bc_in, step_raw, conv_x_state, conv_bc_state, conv_w_x, conv_w_bc,
        dt_bias[None, :], decay_rate[None, :], jnp.repeat(skip_gain, MP)[None, :],
        mixer_gain[None, :], ssm_state.reshape((heads * MP, MN)),
    )
    total = squares + lax.ppermute(squares, "tp", swap)
    scale = lax.rsqrt(total.reshape((row_count, 1)) / DSSM + EPSILON)
    part = mixer_out(gated, scale, w_mixer_out)

    context = attend(seen, queries, fresh_keys, fresh_values, arrived)
    theirs = attn_out(1 - core, context, w_attn_out, part, BF16)
    ours = attn_out(core, context, w_attn_out, part, F32)
    received = lax.ppermute(theirs, "tp", swap)
    mixed = (ours + received.astype(F32)).astype(BF16)
    return (mixed, last_state.reshape(ssm_state.shape))


def solution(mesh):
    return jax.shard_map(
        shards,
        mesh=mesh,
        in_specs=(
            P("req", "tp"),
            P(),
            P(None, "tp"),
            P(None, "tp"),
            P(None, "tp"),
            P("tp", None),
            P("req", None, "tp", None, None),
            P("req", None),
            P("req"),
            P(None, "tp"),
            P(None, "tp"),
            P(),
            P(None, "tp"),
            P(None, "tp"),
            P(),
            P("req", None, "tp"),
            P("req", None, None),
            P("tp"),
            P("tp"),
            P("tp"),
            P("tp"),
            P("tp", None),
            P("req", "tp", None, None),
        ),
        out_specs=(P("req", "tp"), P("req", "tp", None, None)),
        check_vma=False,
    )
```

```python
import functools

import jax
import jax.numpy as jnp
from jax import lax
from jax.experimental import pallas as pl
from jax.experimental.pallas import tpu as pltpu
from jax.sharding import PartitionSpec as P

HEAD_SIZE = 128
MP = 64
MN = 256
DSSM = 1536

EPSILON = 1e-05
ROPE_BASE = 100000.0
NEG_FILL = -1e30
LOG2E = 1.4426950408889634
SCORE_SCALE = HEAD_SIZE ** (-0.5) * LOG2E

VMEM = pl.BlockSpec(memory_space=pltpu.VMEM)
SMEM = pl.BlockSpec(memory_space=pltpu.SMEM)
HBM = pl.BlockSpec(memory_space=pltpu.HBM)
F32 = jnp.float32
BF16 = jnp.bfloat16


def params(mebibytes):
    return pltpu.CompilerParams(vmem_limit_bytes=mebibytes * 2**20)


def rope_tables(token_positions):
    half_width = HEAD_SIZE // 2
    inverse = ROPE_BASE ** (-2.0 * jnp.arange(half_width, dtype=F32) / HEAD_SIZE)
    angles = token_positions.astype(F32)[:, None] * inverse[None, :]
    cosine, sine = jnp.cos(angles), jnp.sin(angles)
    return (
        jnp.concatenate([cosine, cosine], axis=-1),
        jnp.concatenate([-sine, sine], axis=-1),
    )


def want_kernel(pages_dev, capacity, page_size, table_ref, length_ref, want_ref, seen_ref, counts):
    for i in range(counts.shape[0]):
        counts[i] = 0
    for i in range(want_ref.shape[1]):
        want_ref[0, i] = 0
        seen_ref[i] = 0
    for page in range(table_ref.shape[1]):
        entry = table_ref[0, page]
        owner = entry // pages_dev
        rank = counts[owner]
        counts[owner] = rank + 1
        place = owner * capacity + rank
        want_ref[0, place] = entry - owner * pages_dev
        seen_ref[place] = jnp.clip(length_ref[0] - page * page_size, 0, page_size)


def wanted(table, length, devices, pages_dev, page_size):
    capacity = pages_dev // devices
    return pl.pallas_call(
        functools.partial(want_kernel, pages_dev, capacity, page_size),
        out_shape=(
            jax.ShapeDtypeStruct((1, devices * capacity), jnp.int32),
            jax.ShapeDtypeStruct((devices * capacity,), jnp.int32),
        ),
        in_specs=[SMEM, SMEM],
        out_specs=(SMEM, SMEM),
        scratch_shapes=[pltpu.SMEM((devices,), jnp.int32)],
        name="wanted",
    )(table, length)


def share_wants(want, axis, devices):
    low = 1 << ((devices.bit_length() - 1) // 2)

    def swapped(rows, mask):
        return lax.ppermute(rows, axis, [(i, i ^ mask) for i in range(devices)])

    columns = [want] + [swapped(want, j * low) for j in range(1, devices // low)]
    mine = jnp.concatenate(columns, axis=0)
    return [mine] + [swapped(mine, i) for i in range(1, low)]


def gather_kernel(capacity, cuts, low, me_ref, *refs):
    lists, pages_ref = refs[:low], refs[low]
    outs = refs[low + 1 : low + 1 + len(cuts)]
    held, sems_in, sems_out = refs[low + 1 + len(cuts) :]
    high = lists[0].shape[0]
    me = me_ref[0]
    places = []
    for i in range(low):
        for j in range(high):
            for rank in range(capacity):
                slot = lists[i][j, me * capacity + rank]
                target = (me ^ (i + low * j)) * capacity + rank
                index = len(places)
                copy = pltpu.make_async_copy(pages_ref.at[slot], held.at[index], sems_in.at[index])
                copy.start()
                places.append((copy, target))
    sends = []
    for index, (copy, target) in enumerate(places):
        copy.wait()
        for piece, (start, stop) in enumerate(cuts):
            send = pltpu.make_async_copy(
                held.at[index, :, start:stop, :], outs[piece].at[target], sems_out.at[piece, index]
            )
            send.start()
            sends.append(send)
    for send in sends:
        send.wait()


def gather_pages(me, lists, kv_pages, capacity, cuts):
    low = len(lists)
    count = low * lists[0].shape[0] * capacity
    _, two, page_size, width = kv_pages.shape
    return pl.pallas_call(
        functools.partial(gather_kernel, capacity, cuts, low),
        out_shape=tuple(
            jax.ShapeDtypeStruct((count, two, stop - start, width), kv_pages.dtype)
            for start, stop in cuts
        ),
        in_specs=[SMEM] * (low + 1) + [HBM],
        out_specs=(HBM,) * len(cuts),
        scratch_shapes=[
            pltpu.VMEM((count, two, page_size, width), kv_pages.dtype),
            pltpu.SemaphoreType.DMA((count,)),
            pltpu.SemaphoreType.DMA((len(cuts), count)),
        ],
        compiler_params=params(60),
        cost_estimate=pl.CostEstimate(flops=0, bytes_accessed=8 * 2**20, transcendentals=0),
        name="gather_pages",
    )(me, *lists, kv_pages)


def silu(value):
    return value / (1.0 + jnp.exp(-value))


def front_kernel(
    core_ref, mine_ref, other_ref, gain_ref, cos_ref, sin_ref,
    histx_ref, histbc_ref, convx_ref, convbc_ref, bias_ref, rate_ref, skip_ref, mixer_gain_ref,
    wdt_hbm, wbc_hbm, wx_hbm, wz_hbm, wq_hbm, wk_hbm, wv_hbm, state_hbm,
    q_ref, k_ref, v_ref, gated_ref, square_ref, last_hbm,
    normed, wdt, wbc, wx, wz, wq, wkv, state_ref, last_ref, sems,
    x_ref, z_ref, bc_ref, padded, inner, cum, cum_t, step_size, b_ref, c_ref,
):
    copies = [
        pltpu.make_async_copy(source, target, sems.at[i])
        for i, (source, target) in enumerate(
            (
                (wdt_hbm, wdt),
                (wbc_hbm, wbc),
                (wx_hbm, wx),
                (wz_hbm, wz),
                (state_hbm, state_ref),
                (wq_hbm, wq),
                (wk_hbm, wkv.at[:, 0:HEAD_SIZE]),
                (wv_hbm, wkv.at[:, HEAD_SIZE : 2 * HEAD_SIZE]),
            )
        )
    ]
    for copy in copies:
        copy.start()

    rows, half = mine_ref.shape
    core = core_ref[0]
    here = pl.ds(pl.multiple_of(core * half, half), half)
    there = pl.ds(pl.multiple_of((1 - core) * half, half), half)
    step = 64

    def norm_rows(i, carry):
        block = pl.ds(pl.multiple_of(i * step, step), step)
        mine = mine_ref[block, :].astype(F32)
        other = other_ref[block, :].astype(F32)
        total = jnp.sum(mine * mine + other * other, axis=-1, keepdims=True)
        scale = lax.rsqrt(total / (2 * half) + EPSILON)
        normed[block, here] = (mine * scale * gain_ref[:, here]).astype(BF16)
        normed[block, there] = (other * scale * gain_ref[:, there]).astype(BF16)
        return carry

    lax.fori_loop(0, rows // step, norm_rows, 0)

    def dense(weight, target):
        for start in range(0, weight.shape[1], 256):
            tile = slice(start, start + 256)
            target[:, tile] = jnp.dot(
                normed[...], weight[:, tile], preferred_element_type=F32
            ).astype(BF16)

    copies[0].wait()
    raw = lax.dot_general(
        normed[...], wdt[...], (((1,), (1,)), ((), ())), preferred_element_type=F32
    ) + bias_ref[...]
    heads = raw.shape[1]
    copies[1].wait()
    dense(wbc, bc_ref)
    copies[2].wait()
    dense(wx, x_ref)
    copies[3].wait()
    dense(wz, z_ref)

    taps = convx_ref.shape[0]
    group = 2 * MP
    middle = rows // 2

    def conv(history, fresh, kernel):
        width = fresh.shape[1]
        padded[0:8, 0:width] = jnp.zeros((8, width), F32)
        padded[8 - (taps - 1) : 8, 0:width] = history.astype(F32)
        padded[8 : 8 + rows, 0:width] = fresh.astype(F32)
        summed = padded[9 - taps : 9 - taps + rows, 0:width] * kernel[0:1, :]
        for tap in range(1, taps):
            begin = 9 - taps + tap
            summed = summed + padded[begin : begin + rows, 0:width] * kernel[tap : tap + 1, :]
        return silu(summed).astype(BF16)

    for start in range(0, 2 * MN, group):
        part = conv(
            histbc_ref[0, :, start : start + group],
            bc_ref[:, start : start + group],
            convbc_ref[:, start : start + group],
        )
        if start < MN:
            b_ref[:, start : start + group] = part
        else:
            c_ref[:, start - MN : start - MN + group] = part

    size = jnp.maximum(raw, 0.0) + jnp.log1p(jnp.exp(-jnp.abs(raw)))
    step_size[:, 0:heads] = size
    row_index = lax.broadcasted_iota(jnp.int32, (rows, rows), 0)
    column_index = lax.broadcasted_iota(jnp.int32, (rows, rows), 1)
    causal = column_index <= row_index
    cum[...] = jnp.zeros((rows, 128), F32)
    cum[:, 0:heads] = -size * (rate_ref[...] * LOG2E)
    cum[...] = jnp.dot(
        causal.astype(F32), cum[...], precision=lax.Precision.HIGHEST, preferred_element_type=F32
    )
    cum_t[...] = cum[...].T
    inner[...] = jnp.where(
        causal,
        lax.dot_general(c_ref[...], b_ref[...], CONTRACT_LAST, preferred_element_type=F32),
        0.0,
    )
    copies[4].wait()
    first = lax.broadcasted_iota(jnp.int32, (1, group), 1) < MP
    first_rows = lax.broadcasted_iota(jnp.int32, (group, 1), 0) < MP
    squares = jnp.zeros((rows, group), F32)
    for pair in range(heads // 2):
        cols = slice(pair * group, (pair + 1) * group)
        one, two = 2 * pair, 2 * pair + 1
        x_rows = conv(histx_ref[0, :, cols], x_ref[:, cols], convx_ref[:, cols]).astype(F32)
        sizes = jnp.where(first, step_size[:, one : one + 1], step_size[:, two : two + 1])
        fades = jnp.where(first, cum[:, one : one + 1], cum[:, two : two + 1])
        last_fade = fades[rows - 1 : rows, :]
        moved_float = x_rows * sizes
        moved = moved_float.astype(BF16)
        tail_moved = moved_float * jnp.exp2(last_fade - fades)
        state = state_ref[cols, :]
        state_high = state.astype(BF16)
        state_low = (state - state_high.astype(F32)).astype(BF16)
        carried = lax.dot_general(
            c_ref[...], state_high, CONTRACT_LAST, preferred_element_type=F32
        ) + lax.dot_general(c_ref[...], state_low, CONTRACT_LAST, preferred_element_type=F32)
        blocks = []
        for begin in (0, middle):
            end = begin + middle
            sides = []
            for head in (one, two):
                gap = cum[begin:end, head : head + 1] - cum_t[head : head + 1, 0:end]
                mixing = (jnp.exp2(jnp.minimum(gap, 0.0)) * inner[begin:end, 0:end]).astype(BF16)
                sides.append(jnp.dot(mixing, moved[0:end, :], preferred_element_type=F32))
            blocks.append(jnp.where(first, sides[0], sides[1]))
        ssm_y = (
            jnp.concatenate(blocks, axis=0)
            + carried * jnp.exp2(fades)
            + skip_ref[:, cols] * x_rows
        )
        gated = ssm_y * silu(z_ref[:, cols].astype(F32))
        squares = squares + gated * gated
        gated_ref[:, cols] = (gated * mixer_gain_ref[:, cols]).astype(BF16)
        added = jnp.dot(tail_moved.T.astype(BF16), b_ref[...], preferred_element_type=F32)
        ends = jnp.exp2(cum_t[one : two + 1, rows - 1 : rows])
        keep = jnp.where(first_rows, ends[0:1, :], ends[1:2, :])
        last_ref[cols, :] = keep * state + added
    square_ref[...] = jnp.sum(squares.T, axis=0, keepdims=True)
    give_back = pltpu.make_async_copy(last_ref, last_hbm, sems.at[8])
    give_back.start()

    def rope(vectors):
        return vectors * cos_ref[...] + pltpu.roll(vectors, HEAD_SIZE // 2, 1) * sin_ref[...]

    copies[5].wait()
    for tile in range(wq.shape[1] // 256):
        two_heads = jnp.dot(
            normed[...], wq[:, tile * 256 : tile * 256 + 256], preferred_element_type=F32
        )
        for side in range(2):
            head = 2 * tile + side
            q_ref[head * rows : (head + 1) * rows, :] = rope(
                two_heads[:, side * HEAD_SIZE : (side + 1) * HEAD_SIZE]
            ).astype(BF16)
    copies[6].wait()
    copies[7].wait()
    key_value = jnp.dot(normed[...], wkv[...], preferred_element_type=F32)
    k_ref[...] = rope(key_value[:, :HEAD_SIZE]).astype(BF16)
    v_ref[...] = key_value[:, HEAD_SIZE:].astype(BF16)
    give_back.wait()


def front(
    core, mine, other, gain, cosine, sine,
    histx, histbc, convx, convbc, bias, rate, skip, mixer_gain,
    wdt, wbc, wx, wz, wq, wk, wv, state,
):
    rows, half = mine.shape
    width = 2 * half

    def out(shape, dtype=BF16):
        return jax.ShapeDtypeStruct(shape, dtype)

    return pl.pallas_call(
        front_kernel,
        out_shape=(
            out((wq.shape[1] // HEAD_SIZE * rows, HEAD_SIZE)),
            out((rows, wk.shape[1])),
            out((rows, wv.shape[1])),
            out((rows, wx.shape[1])),
            out((1, rows), F32),
            out(state.shape, F32),
        ),
        in_specs=[SMEM] + [VMEM] * 13 + [HBM] * 8,
        out_specs=(VMEM,) * 5 + (HBM,),
        scratch_shapes=[
            pltpu.VMEM((rows, width), BF16),
            pltpu.VMEM(wdt.shape, BF16),
            pltpu.VMEM(wbc.shape, BF16),
            pltpu.VMEM(wx.shape, BF16),
            pltpu.VMEM(wz.shape, BF16),
            pltpu.VMEM(wq.shape, BF16),
            pltpu.VMEM((width, 2 * HEAD_SIZE), BF16),
            pltpu.VMEM(state.shape, F32),
            pltpu.VMEM(state.shape, F32),
            pltpu.SemaphoreType.DMA((9,)),
            pltpu.VMEM((rows, wx.shape[1]), BF16),
            pltpu.VMEM((rows, wz.shape[1]), BF16),
            pltpu.VMEM((rows, wbc.shape[1]), BF16),
            pltpu.VMEM((rows + 8, 2 * MP), F32),
            pltpu.VMEM((rows, rows), F32),
            pltpu.VMEM((rows, 128), F32),
            pltpu.VMEM((128, rows), F32),
            pltpu.VMEM((rows, 128), F32),
            pltpu.VMEM((rows, MN), BF16),
            pltpu.VMEM((rows, MN), BF16),
        ],
        compiler_params=params(32),
        cost_estimate=pl.CostEstimate(
            flops=16 * 10**9, bytes_accessed=17 * 2**20, transcendentals=4 * 10**6
        ),
        name="front",
    )(
        core, mine, other, gain, cosine, sine,
        histx, histbc, convx, convbc, bias, rate, skip, mixer_gain,
        wdt, wbc, wx, wz, wq, wk, wv, state,
    )


CONTRACT_LAST = (((1,), (1,)), ((), ()))
CHUNK = 512


def across(column, width):
    return jnp.concatenate([column] * (width // HEAD_SIZE), axis=1)


def softmax_step(scores, values, state):
    count = scores.shape[1]
    top = jnp.broadcast_to(jnp.max(scores, axis=-1, keepdims=True), (scores.shape[0], HEAD_SIZE))
    if state is not None:
        top = jnp.maximum(state[2], top)
    weights = jnp.exp2((scores - across(top, count)) * SCORE_SCALE).astype(BF16)
    values = jnp.concatenate([values, jnp.ones((count, HEAD_SIZE), BF16)], axis=1)
    added = jnp.dot(weights, values, preferred_element_type=F32)
    summed, total = added[:, :HEAD_SIZE], added[:, HEAD_SIZE:]
    if state is not None:
        fade = jnp.exp2((state[2] - top) * SCORE_SCALE)
        summed, total = state[0] * fade + summed, state[1] * fade + total
    return summed, total, top


def page_step(query, keys, values, seen, state):
    pages, tokens, width = keys.shape
    scores = lax.dot_general(
        query, keys.reshape(pages * tokens, width), CONTRACT_LAST, preferred_element_type=F32
    )
    token = lax.broadcasted_iota(jnp.int32, (1, tokens), 1)
    hide = jnp.concatenate(
        [jnp.where(token >= seen[page], NEG_FILL, 0.0) for page in range(pages)], axis=1
    )
    return softmax_step(scores + hide, values.reshape(pages * tokens, width), state)


def attend_new_kernel(q_ref, k_ref, v_ref, sum_ref, total_ref, top_ref):
    rows = k_ref.shape[0]
    row = lax.broadcasted_iota(jnp.int32, (rows, rows), 0)
    column = lax.broadcasted_iota(jnp.int32, (rows, rows), 1)
    for start in range(0, q_ref.shape[0], rows):
        here = slice(start, start + rows)
        scores = lax.dot_general(
            q_ref[here, :], k_ref[...], CONTRACT_LAST, preferred_element_type=F32
        )
        scores = jnp.where(column <= row, scores, NEG_FILL)
        sum_ref[here, :], total_ref[here, :], top_ref[here, :] = softmax_step(
            scores, v_ref[...], None
        )


def attend_new(queries, keys, values):
    count = queries.shape[0]
    rows = keys.shape[0]
    return pl.pallas_call(
        attend_new_kernel,
        out_shape=(jax.ShapeDtypeStruct((count, HEAD_SIZE), F32),) * 3,
        in_specs=[VMEM] * 3,
        out_specs=(VMEM,) * 3,
        compiler_params=params(16),
        cost_estimate=pl.CostEstimate(
            flops=8 * count * rows * HEAD_SIZE,
            bytes_accessed=4 * 2**20,
            transcendentals=count * rows,
        ),
        name="attend_new",
    )(queries, keys, values)


def attend_pages_kernel(seen_ref, q_ref, sum_ref, total_ref, top_ref, kv_hbm, out_ref, kv_ref, sems):
    pages, _, tokens, _ = kv_ref.shape
    rows = out_ref.shape[0]
    per_chunk = CHUNK // tokens
    spans = [slice(start, start + per_chunk) for start in range(0, pages, per_chunk)]
    copies = [
        pltpu.make_async_copy(kv_hbm.at[span], kv_ref.at[span], sems.at[i])
        for i, span in enumerate(spans)
    ]
    for copy in copies:
        copy.start()
    for head in range(q_ref.shape[0] // rows):
        here = slice(head * rows, (head + 1) * rows)
        query = q_ref[here, :]
        state = (sum_ref[here, :], total_ref[here, :], top_ref[here, :])
        for span, copy in zip(spans, copies):
            if head == 0:
                copy.wait()
            seen = [seen_ref[page] for page in range(span.start, span.stop)]
            state = page_step(query, kv_ref[span, 0], kv_ref[span, 1], seen, state)
        out_ref[:, head * HEAD_SIZE : (head + 1) * HEAD_SIZE] = (state[0] / state[1]).astype(BF16)


def attend_pages(seen, queries, state, kv, rows):
    pages, _, tokens, _ = kv.shape
    count = queries.shape[0]
    return pl.pallas_call(
        attend_pages_kernel,
        out_shape=jax.ShapeDtypeStruct((rows, count // rows * HEAD_SIZE), BF16),
        in_specs=[SMEM] + [VMEM] * 4 + [HBM],
        out_specs=VMEM,
        scratch_shapes=[
            pltpu.VMEM(kv.shape, kv.dtype),
            pltpu.SemaphoreType.DMA((pages * tokens // CHUNK,)),
        ],
        compiler_params=params(16),
        cost_estimate=pl.CostEstimate(
            flops=8 * count * pages * tokens * HEAD_SIZE,
            bytes_accessed=4 * 2**20,
            transcendentals=count * pages * tokens,
        ),
        name="attend_pages",
    )(seen, queries, *state, kv)


def mixer_out_kernel(gated_ref, scale_ref, weight_ref, out_ref):
    for start in range(0, out_ref.shape[1], 256):
        tile = slice(start, start + 256)
        out_ref[:, tile] = (
            jnp.dot(gated_ref[...], weight_ref[:, tile], preferred_element_type=F32)
            * scale_ref[...]
        )


def mixer_out(gated, scale, weight):
    rows, depth = gated.shape
    width = weight.shape[1]
    return pl.pallas_call(
        mixer_out_kernel,
        out_shape=jax.ShapeDtypeStruct((rows, width), F32),
        in_specs=[VMEM] * 3,
        out_specs=VMEM,
        compiler_params=params(16),
        cost_estimate=pl.CostEstimate(
            flops=2 * rows * depth * width, bytes_accessed=8 * 2**20, transcendentals=0
        ),
        name="mixer_out",
    )(gated, scale, weight)


def attn_out_kernel(core_ref, context_ref, weight_ref, part_ref, out_ref):
    half = out_ref.shape[1]
    for start in range(0, half, 256):
        here = pl.ds(pl.multiple_of(core_ref[0] * half + start, 256), 256)
        out_ref[:, start : start + 256] = (
            jnp.dot(context_ref[...], weight_ref[:, here], preferred_element_type=F32)
            + part_ref[:, here]
        ).astype(out_ref.dtype)


def attn_out(core, context, weight, part, dtype):
    rows, depth = context.shape
    half = weight.shape[1] // 2
    return pl.pallas_call(
        attn_out_kernel,
        out_shape=jax.ShapeDtypeStruct((rows, half), dtype),
        in_specs=[SMEM] + [VMEM] * 3,
        out_specs=VMEM,
        compiler_params=params(16),
        cost_estimate=pl.CostEstimate(
            flops=2 * rows * depth * half, bytes_accessed=4 * 2**20, transcendentals=0
        ),
        name="attn_out",
    )(core, context, weight, part)


def shards(
    tokens,
    attn_gain,
    w_query,
    key_weight,
    value_weight,
    w_attn_out,
    kv_pages,
    page_table,
    cached_len,
    w_gate_z,
    w_ssm_in,
    w_bc,
    w_dt,
    conv_w_x,
    conv_w_bc,
    conv_x_state,
    conv_bc_state,
    dt_bias,
    decay_rate,
    skip_gain,
    mixer_gain,
    w_mixer_out,
    ssm_state,
):
    swap = [(0, 1), (1, 0)]
    core = lax.axis_index("tp").astype(jnp.int32).reshape(1)
    row_count = tokens.shape[0]
    devices = lax.axis_size("req")
    pages_dev = kv_pages.shape[0]
    capacity = pages_dev // devices
    page_size = kv_pages.shape[3]
    length = cached_len[0]

    want, seen = wanted(page_table, cached_len, devices, pages_dev, page_size)
    cosine, sine = rope_tables(length + jnp.arange(row_count, dtype=jnp.int32))
    other = lax.ppermute(tokens, "tp", swap)
    lists = share_wants(want, "req", devices)
    me = lax.axis_index("req").astype(jnp.int32).reshape(1)
    cuts = ((0, page_size),)
    fetched = gather_pages(
        me, lists, kv_pages.reshape((pages_dev, 2, page_size, HEAD_SIZE)), capacity, cuts
    )

    arrived = lax.all_to_all(
        fetched[0].reshape((devices, capacity) + fetched[0].shape[1:]),
        "req",
        split_axis=0,
        concat_axis=0,
        tiled=True,
    ).reshape(fetched[0].shape)

    heads = w_dt.shape[1]
    queries, fresh_keys, fresh_values, gated, squares, last_state = front(
        core, tokens, other, attn_gain[None, :], cosine, sine,
        conv_x_state, conv_bc_state, conv_w_x, conv_w_bc,
        dt_bias[None, :], decay_rate[None, :], jnp.repeat(skip_gain, MP)[None, :],
        mixer_gain[None, :],
        w_dt.T, w_bc, w_ssm_in, w_gate_z, w_query, key_weight, value_weight,
        ssm_state.reshape((heads * MP, MN)),
    )
    total = squares + lax.ppermute(squares, "tp", swap)
    scale = lax.rsqrt(total.reshape((row_count, 1)) / DSSM + EPSILON)
    part = mixer_out(gated, scale, w_mixer_out)
    state = attend_new(queries, fresh_keys, fresh_values)
    context = attend_pages(seen, queries, state, arrived, row_count)
    theirs = attn_out(1 - core, context, w_attn_out, part, BF16)
    ours = attn_out(core, context, w_attn_out, part, F32)
    received = lax.ppermute(theirs, "tp", swap)
    mixed = (ours + received.astype(F32)).astype(BF16)
    return (mixed, last_state.reshape(ssm_state.shape))


def solution(mesh):
    return jax.shard_map(
        shards,
        mesh=mesh,
        in_specs=(
            P("req", "tp"),
            P(),
            P(None, "tp"),
            P(None, "tp"),
            P(None, "tp"),
            P("tp", None),
            P("req", None, "tp", None, None),
            P("req", None),
            P("req"),
            P(None, "tp"),
            P(None, "tp"),
            P(),
            P(None, "tp"),
            P(None, "tp"),
            P(),
            P("req", None, "tp"),
            P("req", None, None),
            P("tp"),
            P("tp"),
            P("tp"),
            P("tp"),
            P("tp", None),
            P("req", "tp", None, None),
        ),
        out_specs=(P("req", "tp"), P("req", "tp", None, None)),
        check_vma=False,
    )
```

```python
import functools

import jax
import jax.numpy as jnp
from jax import lax
from jax.experimental import pallas as pl
from jax.experimental.pallas import tpu as pltpu
from jax.sharding import PartitionSpec as P

HEAD_SIZE = 128
MP = 64
MN = 256
DSSM = 1536

EPSILON = 1e-05
ROPE_BASE = 100000.0
NEG_FILL = -1e30
LOG2E = 1.4426950408889634
SCORE_SCALE = HEAD_SIZE ** (-0.5) * LOG2E

VMEM = pl.BlockSpec(memory_space=pltpu.VMEM)
SMEM = pl.BlockSpec(memory_space=pltpu.SMEM)
HBM = pl.BlockSpec(memory_space=pltpu.HBM)
F32 = jnp.float32
BF16 = jnp.bfloat16
LIGHT = pl.CostEstimate(flops=10**6, bytes_accessed=10**4, transcendentals=0)


def params(mebibytes):
    return pltpu.CompilerParams(vmem_limit_bytes=mebibytes * 2**20)


def rope_tables(token_positions):
    half_width = HEAD_SIZE // 2
    inverse = ROPE_BASE ** (-2.0 * jnp.arange(half_width, dtype=F32) / HEAD_SIZE)
    angles = token_positions.astype(F32)[:, None] * inverse[None, :]
    cosine, sine = jnp.cos(angles), jnp.sin(angles)
    return (
        jnp.concatenate([cosine, cosine], axis=-1),
        jnp.concatenate([-sine, sine], axis=-1),
    )


def want_kernel(pages_dev, capacity, page_size, table_ref, length_ref, want_ref, seen_ref, slots, counts):
    for i in range(counts.shape[0]):
        counts[i] = 0
    for i in range(slots.shape[0]):
        slots[i] = 0
        seen_ref[i] = 0
    for page in range(table_ref.shape[1]):
        entry = table_ref[0, page]
        owner = entry // pages_dev
        rank = counts[owner]
        counts[owner] = rank + 1
        place = owner * capacity + rank
        slots[place] = entry - owner * pages_dev
        seen_ref[place] = jnp.clip(length_ref[0] - page * page_size, 0, page_size)
    lane = lax.broadcasted_iota(jnp.int32, want_ref.shape[1:], 1)
    for owner in range(want_ref.shape[0]):
        tile = jnp.zeros(want_ref.shape[1:], jnp.int32)
        for rank in range(capacity):
            tile = jnp.where(lane == rank, slots[owner * capacity + rank], tile)
        want_ref[owner] = tile


def wanted(table, length, devices, pages_dev, page_size):
    capacity = pages_dev // devices
    return pl.pallas_call(
        functools.partial(want_kernel, pages_dev, capacity, page_size),
        out_shape=(
            jax.ShapeDtypeStruct((devices, 8, 128), jnp.int32),
            jax.ShapeDtypeStruct((devices * capacity,), jnp.int32),
        ),
        in_specs=[SMEM, SMEM],
        out_specs=(VMEM, SMEM),
        scratch_shapes=[
            pltpu.SMEM((devices * capacity,), jnp.int32),
            pltpu.SMEM((devices,), jnp.int32),
        ],
        name="wanted",
    )(table, length)


def gather_kernel(capacity, asked_hbm, pages_ref, out_ref, own_ref, asked, held, sem, sems_in, sems_out):
    me = lax.axis_index("req")
    load = pltpu.make_async_copy(asked_hbm, asked, sem.at[0])
    load.start()
    load.wait()
    count = held.shape[0]
    reads = []
    for index in range(count):
        slot = asked[index // capacity, 0, index % capacity]
        reads.append(
            pltpu.make_async_copy(pages_ref.at[slot], held.at[index], sems_in.at[index])
        )
        reads[-1].start()
    writes = []
    for index in range(count):
        reads[index].wait()
        writes.append(
            pltpu.make_async_copy(held.at[index], out_ref.at[index], sems_out.at[index])
        )
        writes[-1].start()
    mine = pltpu.make_async_copy(held.at[pl.ds(me * capacity, capacity)], own_ref, sem.at[1])
    mine.start()
    for write in writes:
        write.wait()
    mine.wait()


def gather_pages(asked, kv_pages, capacity):
    count = asked.shape[0] * capacity
    page = kv_pages.shape[1:]
    return pl.pallas_call(
        functools.partial(gather_kernel, capacity),
        out_shape=(
            jax.ShapeDtypeStruct((count,) + page, kv_pages.dtype),
            jax.ShapeDtypeStruct((capacity,) + page, kv_pages.dtype),
        ),
        in_specs=[HBM, HBM],
        out_specs=(HBM, HBM),
        scratch_shapes=[
            pltpu.SMEM(asked.shape, jnp.int32),
            pltpu.VMEM((count,) + page, kv_pages.dtype),
            pltpu.SemaphoreType.DMA((2,)),
            pltpu.SemaphoreType.DMA((count,)),
            pltpu.SemaphoreType.DMA((count,)),
        ],
        compiler_params=params(60),
        cost_estimate=LIGHT,
        name="gather_pages",
    )(asked, kv_pages)


def silu(value):
    return value / (1.0 + jnp.exp(-value))


def front_kernel(
    core_ref, mine_ref, other_ref, gain_ref, cos_ref, sin_ref,
    histx_ref, histbc_ref, convx_ref, convbc_ref, bias_ref, rate_ref, skip_ref, mixer_gain_ref,
    wdt_hbm, wbc_hbm, wx_hbm, wz_hbm, wq_hbm, wk_hbm, wv_hbm, state_hbm,
    q_ref, k_ref, v_ref, gated_ref, square_ref, last_hbm,
    normed, wdt, wbc, wx, wz, wq, wkv, state_ref, last_ref, sems,
    x_ref, z_ref, bc_ref, padded, inner, cum, cum_t, step_size, b_ref, c_ref,
):
    copies = [
        pltpu.make_async_copy(source, target, sems.at[i])
        for i, (source, target) in enumerate(
            (
                (wdt_hbm, wdt),
                (wbc_hbm, wbc),
                (wx_hbm, wx),
                (wz_hbm, wz),
                (state_hbm, state_ref),
                (wq_hbm, wq),
                (wk_hbm, wkv.at[:, 0:HEAD_SIZE]),
                (wv_hbm, wkv.at[:, HEAD_SIZE : 2 * HEAD_SIZE]),
            )
        )
    ]
    for copy in copies:
        copy.start()

    rows, half = mine_ref.shape
    core = core_ref[0]
    here = pl.ds(pl.multiple_of(core * half, half), half)
    there = pl.ds(pl.multiple_of((1 - core) * half, half), half)
    step = 64

    def norm_rows(i, carry):
        block = pl.ds(pl.multiple_of(i * step, step), step)
        mine = mine_ref[block, :].astype(F32)
        other = other_ref[block, :].astype(F32)
        total = jnp.sum(mine * mine + other * other, axis=-1, keepdims=True)
        scale = lax.rsqrt(total / (2 * half) + EPSILON)
        normed[block, here] = (mine * scale * gain_ref[:, here]).astype(BF16)
        normed[block, there] = (other * scale * gain_ref[:, there]).astype(BF16)
        return carry

    lax.fori_loop(0, rows // step, norm_rows, 0)

    def dense(weight, target):
        for start in range(0, weight.shape[1], 256):
            tile = slice(start, start + 256)
            target[:, tile] = jnp.dot(
                normed[...], weight[:, tile], preferred_element_type=F32
            ).astype(BF16)

    copies[0].wait()
    raw = lax.dot_general(
        normed[...], wdt[...], (((1,), (1,)), ((), ())), preferred_element_type=F32
    ) + bias_ref[...]
    heads = raw.shape[1]
    copies[1].wait()
    dense(wbc, bc_ref)
    copies[2].wait()
    dense(wx, x_ref)
    copies[3].wait()
    dense(wz, z_ref)

    taps = convx_ref.shape[0]
    group = 2 * MP
    middle = rows // 2

    def conv(history, fresh, kernel):
        width = fresh.shape[1]
        padded[0:8, 0:width] = jnp.zeros((8, width), F32)
        padded[8 - (taps - 1) : 8, 0:width] = history.astype(F32)
        padded[8 : 8 + rows, 0:width] = fresh.astype(F32)
        summed = padded[9 - taps : 9 - taps + rows, 0:width] * kernel[0:1, :]
        for tap in range(1, taps):
            begin = 9 - taps + tap
            summed = summed + padded[begin : begin + rows, 0:width] * kernel[tap : tap + 1, :]
        return silu(summed).astype(BF16)

    for start in range(0, 2 * MN, group):
        part = conv(
            histbc_ref[0, :, start : start + group],
            bc_ref[:, start : start + group],
            convbc_ref[:, start : start + group],
        )
        if start < MN:
            b_ref[:, start : start + group] = part
        else:
            c_ref[:, start - MN : start - MN + group] = part

    size = jnp.maximum(raw, 0.0) + jnp.log1p(jnp.exp(-jnp.abs(raw)))
    step_size[:, 0:heads] = size
    row_index = lax.broadcasted_iota(jnp.int32, (rows, rows), 0)
    column_index = lax.broadcasted_iota(jnp.int32, (rows, rows), 1)
    causal = column_index <= row_index
    cum[...] = jnp.zeros((rows, 128), F32)
    cum[:, 0:heads] = -size * (rate_ref[...] * LOG2E)
    cum[...] = jnp.dot(
        causal.astype(F32), cum[...], precision=lax.Precision.HIGHEST, preferred_element_type=F32
    )
    cum_t[...] = cum[...].T
    inner[...] = jnp.where(
        causal,
        lax.dot_general(c_ref[...], b_ref[...], CONTRACT_LAST, preferred_element_type=F32),
        0.0,
    )
    copies[4].wait()
    first = lax.broadcasted_iota(jnp.int32, (1, group), 1) < MP
    first_rows = lax.broadcasted_iota(jnp.int32, (group, 1), 0) < MP
    squares = jnp.zeros((rows, group), F32)
    for pair in range(heads // 2):
        cols = slice(pair * group, (pair + 1) * group)
        one, two = 2 * pair, 2 * pair + 1
        x_rows = conv(histx_ref[0, :, cols], x_ref[:, cols], convx_ref[:, cols]).astype(F32)
        sizes = jnp.where(first, step_size[:, one : one + 1], step_size[:, two : two + 1])
        fades = jnp.where(first, cum[:, one : one + 1], cum[:, two : two + 1])
        last_fade = fades[rows - 1 : rows, :]
        moved_float = x_rows * sizes
        moved = moved_float.astype(BF16)
        tail_moved = moved_float * jnp.exp2(last_fade - fades)
        state = state_ref[cols, :]
        state_high = state.astype(BF16)
        state_low = (state - state_high.astype(F32)).astype(BF16)
        carried = lax.dot_general(
            c_ref[...], state_high, CONTRACT_LAST, preferred_element_type=F32
        ) + lax.dot_general(c_ref[...], state_low, CONTRACT_LAST, preferred_element_type=F32)
        blocks = []
        for begin in (0, middle):
            end = begin + middle
            sides = []
            for head in (one, two):
                gap = cum[begin:end, head : head + 1] - cum_t[head : head + 1, 0:end]
                mixing = (jnp.exp2(jnp.minimum(gap, 0.0)) * inner[begin:end, 0:end]).astype(BF16)
                sides.append(jnp.dot(mixing, moved[0:end, :], preferred_element_type=F32))
            blocks.append(jnp.where(first, sides[0], sides[1]))
        ssm_y = (
            jnp.concatenate(blocks, axis=0)
            + carried * jnp.exp2(fades)
            + jnp.where(first, skip_ref[one], skip_ref[two]) * x_rows
        )
        gated = ssm_y * silu(z_ref[:, cols].astype(F32))
        squares = squares + gated * gated
        gated_ref[:, cols] = (gated * mixer_gain_ref[:, cols]).astype(BF16)
        added = jnp.dot(tail_moved.T.astype(BF16), b_ref[...], preferred_element_type=F32)
        ends = jnp.exp2(cum_t[one : two + 1, rows - 1 : rows])
        keep = jnp.where(first_rows, ends[0:1, :], ends[1:2, :])
        last_ref[cols, :] = keep * state + added
    square_ref[...] = jnp.sum(squares.T, axis=0, keepdims=True)
    give_back = pltpu.make_async_copy(last_ref, last_hbm, sems.at[8])
    give_back.start()

    def rope(vectors):
        return vectors * cos_ref[...] + pltpu.roll(vectors, HEAD_SIZE // 2, 1) * sin_ref[...]

    copies[5].wait()
    for tile in range(wq.shape[1] // 256):
        two_heads = jnp.dot(
            normed[...], wq[:, tile * 256 : tile * 256 + 256], preferred_element_type=F32
        )
        for side in range(2):
            head = 2 * tile + side
            q_ref[head * rows : (head + 1) * rows, :] = rope(
                two_heads[:, side * HEAD_SIZE : (side + 1) * HEAD_SIZE]
            ).astype(BF16)
    copies[6].wait()
    copies[7].wait()
    key_value = jnp.dot(normed[...], wkv[...], preferred_element_type=F32)
    k_ref[...] = rope(key_value[:, :HEAD_SIZE]).astype(BF16)
    v_ref[...] = key_value[:, HEAD_SIZE:].astype(BF16)
    give_back.wait()


def front(
    core, mine, other, gain, cosine, sine,
    histx, histbc, convx, convbc, bias, rate, skip, mixer_gain,
    wdt, wbc, wx, wz, wq, wk, wv, state,
):
    rows, half = mine.shape
    width = 2 * half

    def out(shape, dtype=BF16):
        return jax.ShapeDtypeStruct(shape, dtype)

    return pl.pallas_call(
        front_kernel,
        out_shape=(
            out((wq.shape[1] // HEAD_SIZE * rows, HEAD_SIZE)),
            out((rows, wk.shape[1])),
            out((rows, wv.shape[1])),
            out((rows, wx.shape[1])),
            out((1, rows), F32),
            out(state.shape, F32),
        ),
        in_specs=[SMEM] + [VMEM] * 11 + [SMEM, VMEM] + [HBM] * 8,
        out_specs=(VMEM,) * 5 + (HBM,),
        scratch_shapes=[
            pltpu.VMEM((rows, width), BF16),
            pltpu.VMEM(wdt.shape, BF16),
            pltpu.VMEM(wbc.shape, BF16),
            pltpu.VMEM(wx.shape, BF16),
            pltpu.VMEM(wz.shape, BF16),
            pltpu.VMEM(wq.shape, BF16),
            pltpu.VMEM((width, 2 * HEAD_SIZE), BF16),
            pltpu.VMEM(state.shape, F32),
            pltpu.VMEM(state.shape, F32),
            pltpu.SemaphoreType.DMA((9,)),
            pltpu.VMEM((rows, wx.shape[1]), BF16),
            pltpu.VMEM((rows, wz.shape[1]), BF16),
            pltpu.VMEM((rows, wbc.shape[1]), BF16),
            pltpu.VMEM((rows + 8, 2 * MP), F32),
            pltpu.VMEM((rows, rows), F32),
            pltpu.VMEM((rows, 128), F32),
            pltpu.VMEM((128, rows), F32),
            pltpu.VMEM((rows, 128), F32),
            pltpu.VMEM((rows, MN), BF16),
            pltpu.VMEM((rows, MN), BF16),
        ],
        compiler_params=params(60),
        cost_estimate=LIGHT,
        name="front",
    )(
        core, mine, other, gain, cosine, sine,
        histx, histbc, convx, convbc, bias, rate, skip, mixer_gain,
        wdt, wbc, wx, wz, wq, wk, wv, state,
    )


CONTRACT_LAST = (((1,), (1,)), ((), ()))
CHUNK = 512


def across(column, width):
    return jnp.concatenate([column] * (width // HEAD_SIZE), axis=1)


def softmax_step(scores, values, state):
    count = scores.shape[1]
    top = jnp.broadcast_to(jnp.max(scores, axis=-1, keepdims=True), (scores.shape[0], HEAD_SIZE))
    if state is not None:
        top = jnp.maximum(state[2], top)
    weights = jnp.exp2((scores - across(top, count)) * SCORE_SCALE).astype(BF16)
    values = jnp.concatenate([values, jnp.ones((count, HEAD_SIZE), BF16)], axis=1)
    added = jnp.dot(weights, values, preferred_element_type=F32)
    summed, total = added[:, :HEAD_SIZE], added[:, HEAD_SIZE:]
    if state is not None:
        fade = jnp.exp2((state[2] - top) * SCORE_SCALE)
        summed, total = state[0] * fade + summed, state[1] * fade + total
    return summed, total, top


def page_step(query, keys, values, seen, state):
    pages, tokens, width = keys.shape
    scores = lax.dot_general(
        query, keys.reshape(pages * tokens, width), CONTRACT_LAST, preferred_element_type=F32
    )
    token = lax.broadcasted_iota(jnp.int32, (1, tokens), 1)
    hide = jnp.concatenate(
        [jnp.where(token >= seen[page], NEG_FILL, 0.0) for page in range(pages)], axis=1
    )
    return softmax_step(scores + hide, values.reshape(pages * tokens, width), state)


def attend_early_kernel(masks, picks, fresh, seen_ref, q_hbm, *refs):
    count = max(array for array, _ in picks) + 1
    given = 2 if fresh else 3
    start_hbm, arrays = refs[:given], refs[given : given + count]
    outs = refs[given + count : given + count + 3]
    q_ref, k_ref, v_ref, kv_ref, states, sems, sems_out = refs[given + count + 3 :]
    rows = k_ref.shape[0]
    pages, _, tokens, _ = kv_ref.shape
    capacity = pages // len(masks)
    me = lax.axis_index("req")
    targets = (k_ref, v_ref) if fresh else (states.at[0], states.at[1], states.at[2])
    copies = [pltpu.make_async_copy(q_hbm, q_ref, sems.at[0])]
    for index, (source, target) in enumerate(zip(start_hbm, targets)):
        copies.append(pltpu.make_async_copy(source, target, sems.at[1 + index]))
    for index, (array, entry) in enumerate(picks):
        source = arrays[array] if entry is None else arrays[array].at[entry]
        copies.append(
            pltpu.make_async_copy(
                source, kv_ref.at[pl.ds(index * capacity, capacity)], sems.at[4 + index]
            )
        )
    for copy in copies:
        copy.start()
    seen = [seen_ref[(me ^ mask) * capacity + rank] for mask in masks for rank in range(capacity)]
    row = lax.broadcasted_iota(jnp.int32, (rows, rows), 0)
    column = lax.broadcasted_iota(jnp.int32, (rows, rows), 1)
    for copy in copies:
        copy.wait()
    per_chunk = CHUNK // tokens
    sends = []
    for head, start in enumerate(range(0, q_ref.shape[0], rows)):
        here = slice(start, start + rows)
        if fresh:
            scores = lax.dot_general(
                q_ref[here, :], k_ref[...], CONTRACT_LAST, preferred_element_type=F32
            )
            state = softmax_step(jnp.where(column <= row, scores, NEG_FILL), v_ref[...], None)
        else:
            state = (states[0, here, :], states[1, here, :], states[2, here, :])
        for begin in range(0, pages, per_chunk):
            span = slice(begin, begin + per_chunk)
            state = page_step(q_ref[here, :], kv_ref[span, 0], kv_ref[span, 1], seen[span], state)
        for kind in range(3):
            states[kind, here, :] = state[kind]
            send = pltpu.make_async_copy(
                states.at[kind, here, :], outs[kind].at[here, :], sems_out.at[3 * head + kind]
            )
            send.start()
            sends.append(send)
    for send in sends:
        send.wait()


def attend_early(seen, queries, start, rows, arrays, masks, picks):
    count = queries.shape[0]
    block = arrays[0].shape[-4:]
    pages = len(masks) * block[0]
    fresh = len(start) == 2
    return pl.pallas_call(
        functools.partial(attend_early_kernel, masks, picks, fresh),
        out_shape=(jax.ShapeDtypeStruct((count, HEAD_SIZE), F32),) * 3,
        in_specs=[SMEM] + [HBM] * (1 + len(start) + len(arrays)),
        out_specs=(HBM,) * 3,
        scratch_shapes=[
            pltpu.VMEM(queries.shape, BF16),
            pltpu.VMEM((rows, HEAD_SIZE), BF16),
            pltpu.VMEM((rows, HEAD_SIZE), BF16),
            pltpu.VMEM((pages,) + block[1:], BF16),
            pltpu.VMEM((3, count, HEAD_SIZE), F32),
            pltpu.SemaphoreType.DMA((4 + len(masks),)),
            pltpu.SemaphoreType.DMA((3 * count // rows,)),
        ],
        compiler_params=params(60),
        cost_estimate=LIGHT,
        name="attend_first" if fresh else "attend_more",
    )(seen, queries, *start, *arrays)


def attend_late_kernel(
    masks, core_ref, seen_ref, q_hbm, sum_hbm, total_hbm, top_hbm, weight_hbm, part_hbm, kv_hbm,
    context_ref, out_ref, q_ref, near, far, kv_ref, weight_ref, part_ref, sems, sems_late,
):
    pages, _, tokens, _ = kv_ref.shape
    capacity = pages // len(masks)
    me = lax.axis_index("req")
    rows, half = out_ref.shape
    heads = q_ref.shape[0] // rows
    per_chunk = CHUNK // tokens
    now = [pltpu.make_async_copy(q_hbm, q_ref, sems.at[0])] + [
        pltpu.make_async_copy(
            kv_hbm.at[pl.ds((me ^ mask) * capacity, capacity)],
            kv_ref.at[pl.ds(index * capacity, capacity)],
            sems.at[1 + index],
        )
        for index, mask in enumerate(masks)
    ]
    there = pl.ds(pl.multiple_of((1 - core_ref[0]) * half, half), half)
    late = [
        pltpu.make_async_copy(source, near.at[kind], sems_late.at[kind])
        for kind, source in enumerate((sum_hbm, total_hbm, top_hbm))
    ] + [
        pltpu.make_async_copy(weight_hbm.at[:, there], weight_ref, sems_late.at[3]),
        pltpu.make_async_copy(part_hbm, part_ref, sems_late.at[4]),
    ]
    for copy in now:
        copy.start()
    seen = [seen_ref[(me ^ mask) * capacity + rank] for mask in masks for rank in range(capacity)]
    for copy in now:
        copy.wait()
    for copy in late:
        copy.start()
    for head in range(heads):
        here = slice(head * rows, (head + 1) * rows)
        state = None
        for begin in range(0, pages, per_chunk):
            span = slice(begin, begin + per_chunk)
            state = page_step(q_ref[here, :], kv_ref[span, 0], kv_ref[span, 1], seen[span], state)
        for kind in range(3):
            far[kind, here, :] = state[kind]
    for copy in late:
        copy.wait()
    for head in range(heads):
        here = slice(head * rows, (head + 1) * rows)
        top = jnp.maximum(near[2, here, :], far[2, here, :])
        fade_near = jnp.exp2((near[2, here, :] - top) * SCORE_SCALE)
        fade_far = jnp.exp2((far[2, here, :] - top) * SCORE_SCALE)
        summed = near[0, here, :] * fade_near + far[0, here, :] * fade_far
        total = near[1, here, :] * fade_near + far[1, here, :] * fade_far
        context_ref[:, head * HEAD_SIZE : (head + 1) * HEAD_SIZE] = (summed / total).astype(BF16)
    for start in range(0, half, 256):
        tile = slice(start, start + 256)
        out_ref[:, tile] = (
            jnp.dot(context_ref[...], weight_ref[:, tile], preferred_element_type=F32)
            + part_ref[:, tile]
        ).astype(BF16)


def attend_late(core, seen, queries, state, weight, part, kv, masks):
    rows, half = part.shape
    count = queries.shape[0]
    pages = len(masks) * kv.shape[0] // lax.axis_size("req")
    return pl.pallas_call(
        functools.partial(attend_late_kernel, masks),
        out_shape=(
            jax.ShapeDtypeStruct((rows, count // rows * HEAD_SIZE), BF16),
            jax.ShapeDtypeStruct((rows, half), BF16),
        ),
        in_specs=[SMEM] * 2 + [HBM] * 7,
        out_specs=(VMEM, VMEM),
        scratch_shapes=[
            pltpu.VMEM(queries.shape, BF16),
            pltpu.VMEM((3, count, HEAD_SIZE), F32),
            pltpu.VMEM((3, count, HEAD_SIZE), F32),
            pltpu.VMEM((pages,) + kv.shape[1:], BF16),
            pltpu.VMEM((weight.shape[0], half), BF16),
            pltpu.VMEM((rows, half), F32),
            pltpu.SemaphoreType.DMA((1 + len(masks),)),
            pltpu.SemaphoreType.DMA((5,)),
        ],
        compiler_params=params(60),
        cost_estimate=LIGHT,
        name="attend_late",
    )(core, seen, queries, *state, weight, part, kv)


def mixer_out_kernel(core_ref, gated_ref, scale_ref, weight_ref, theirs_ref, ours_ref):
    half = ours_ref.shape[1]
    for start in range(0, half, 256):
        for core, out_ref in ((1 - core_ref[0], theirs_ref), (core_ref[0], ours_ref)):
            here = pl.ds(pl.multiple_of(core * half + start, 256), 256)
            out_ref[:, start : start + 256] = (
                jnp.dot(gated_ref[...], weight_ref[:, here], preferred_element_type=F32)
                * scale_ref[...]
            )


def mixer_out(core, gated, scale, weight):
    rows, depth = gated.shape
    width = weight.shape[1]
    return pl.pallas_call(
        mixer_out_kernel,
        out_shape=(jax.ShapeDtypeStruct((rows, width // 2), F32),) * 2,
        in_specs=[SMEM] + [VMEM] * 3,
        out_specs=(VMEM,) * 2,
        compiler_params=params(16),
        cost_estimate=LIGHT,
        name="mixer_out",
    )(core, gated, scale, weight)


def ours_kernel(core_ref, context_ref, weight_ref, part_ref, out_ref):
    half = out_ref.shape[1]
    for start in range(0, half, 256):
        here = pl.ds(pl.multiple_of(core_ref[0] * half + start, 256), 256)
        tile = slice(start, start + 256)
        out_ref[:, tile] = (
            jnp.dot(context_ref[...], weight_ref[:, here], preferred_element_type=F32)
            + part_ref[:, tile]
        )


def ours_half(core, context, weight, part):
    rows, depth = context.shape
    half = weight.shape[1] // 2
    return pl.pallas_call(
        ours_kernel,
        out_shape=jax.ShapeDtypeStruct((rows, half), F32),
        in_specs=[SMEM] + [VMEM] * 3,
        out_specs=VMEM,
        compiler_params=params(16),
        cost_estimate=LIGHT,
        name="ours_half",
    )(core, context, weight, part)


def shards(
    tokens,
    attn_gain,
    w_query,
    key_weight,
    value_weight,
    w_attn_out,
    kv_pages,
    page_table,
    cached_len,
    w_gate_z,
    w_ssm_in,
    w_bc,
    w_dt,
    conv_w_x,
    conv_w_bc,
    conv_x_state,
    conv_bc_state,
    dt_bias,
    decay_rate,
    skip_gain,
    mixer_gain,
    w_mixer_out,
    ssm_state,
):
    swap = [(0, 1), (1, 0)]
    core = lax.axis_index("tp").astype(jnp.int32).reshape(1)
    row_count = tokens.shape[0]
    devices = lax.axis_size("req")
    pages_dev = kv_pages.shape[0]
    capacity = pages_dev // devices
    page_size = kv_pages.shape[3]
    length = cached_len[0]

    want, seen = wanted(page_table, cached_len, devices, pages_dev, page_size)
    cosine, sine = rope_tables(length + jnp.arange(row_count, dtype=jnp.int32))
    other = lax.ppermute(tokens, "tp", swap)

    def exchange(blocks):
        return lax.all_to_all(blocks, "req", split_axis=0, concat_axis=0, tiled=True)

    fetched, own = gather_pages(
        exchange(want), kv_pages.reshape((pages_dev, 2, page_size, HEAD_SIZE)), capacity
    )
    arrived = exchange(fetched.reshape((devices, capacity) + fetched.shape[1:])).reshape(
        fetched.shape
    )

    heads = w_dt.shape[1]
    queries, fresh_keys, fresh_values, gated, squares, last_state = front(
        core, tokens, other, attn_gain[None, :], cosine, sine,
        conv_x_state, conv_bc_state, conv_w_x, conv_w_bc,
        dt_bias[None, :], decay_rate[None, :], skip_gain,
        mixer_gain[None, :],
        w_dt.T, w_bc, w_ssm_in, w_gate_z, w_query, key_weight, value_weight,
        ssm_state.reshape((heads * MP, MN)),
    )
    total = squares + lax.ppermute(squares, "tp", swap)
    scale = lax.rsqrt(total.reshape((row_count, 1)) / DSSM + EPSILON)
    part_theirs, part_ours = mixer_out(core, gated, scale, w_mixer_out)
    state = attend_early(
        seen, queries, (fresh_keys, fresh_values), row_count, [own], [0], [(0, None)]
    )
    context, theirs = attend_late(
        core, seen, queries, state, w_attn_out, part_theirs, arrived, list(range(1, devices))
    )
    received = lax.ppermute(theirs, "tp", swap)
    ours = ours_half(core, context, w_attn_out, part_ours)
    mixed = (ours + received.astype(F32)).astype(BF16)
    return (mixed, last_state.reshape(ssm_state.shape))


def solution(mesh):
    return jax.shard_map(
        shards,
        mesh=mesh,
        in_specs=(
            P("req", "tp"),
            P(),
            P(None, "tp"),
            P(None, "tp"),
            P(None, "tp"),
            P("tp", None),
            P("req", None, "tp", None, None),
            P("req", None),
            P("req"),
            P(None, "tp"),
            P(None, "tp"),
            P(),
            P(None, "tp"),
            P(None, "tp"),
            P(),
            P("req", None, "tp"),
            P("req", None, None),
            P("tp"),
            P("tp"),
            P("tp"),
            P("tp"),
            P("tp", None),
            P("req", "tp", None, None),
        ),
        out_specs=(P("req", "tp"), P("req", "tp", None, None)),
        check_vma=False,
    )
```

```python
import functools

import jax
import jax.numpy as jnp
from jax import lax
from jax.experimental import pallas as pl
from jax.experimental.pallas import tpu as pltpu
from jax.sharding import PartitionSpec as P

HEAD_SIZE = 128
MP = 64
MN = 256
DSSM = 1536

EPSILON = 1e-05
ROPE_BASE = 100000.0
NEG_FILL = -1e30
LOG2E = 1.4426950408889634
SCORE_SCALE = HEAD_SIZE ** (-0.5) * LOG2E

VMEM = pl.BlockSpec(memory_space=pltpu.VMEM)
SMEM = pl.BlockSpec(memory_space=pltpu.SMEM)
HBM = pl.BlockSpec(memory_space=pltpu.HBM)
F32 = jnp.float32
BF16 = jnp.bfloat16
LIGHT = pl.CostEstimate(flops=10**6, bytes_accessed=10**4, transcendentals=0)


def params(mebibytes):
    return pltpu.CompilerParams(vmem_limit_bytes=mebibytes * 2**20)


def rope_tables(token_positions):
    half_width = HEAD_SIZE // 2
    inverse = ROPE_BASE ** (-2.0 * jnp.arange(half_width, dtype=F32) / HEAD_SIZE)
    angles = token_positions.astype(F32)[:, None] * inverse[None, :]
    cosine, sine = jnp.cos(angles), jnp.sin(angles)
    return (
        jnp.concatenate([cosine, cosine], axis=-1),
        jnp.concatenate([-sine, sine], axis=-1),
    )


def want_kernel(pages_dev, capacity, page_size, table_ref, length_ref, want_ref, seen_ref, slots, counts):
    for i in range(counts.shape[0]):
        counts[i] = 0
    for i in range(slots.shape[0]):
        slots[i] = 0
        seen_ref[i] = 0
    for page in range(table_ref.shape[1]):
        entry = table_ref[0, page]
        owner = entry // pages_dev
        rank = counts[owner]
        counts[owner] = rank + 1
        place = owner * capacity + rank
        slots[place] = entry - owner * pages_dev
        seen_ref[place] = jnp.clip(length_ref[0] - page * page_size, 0, page_size)
    lane = lax.broadcasted_iota(jnp.int32, want_ref.shape[1:], 1)
    for owner in range(want_ref.shape[0]):
        tile = jnp.zeros(want_ref.shape[1:], jnp.int32)
        for rank in range(capacity):
            tile = jnp.where(lane == rank, slots[owner * capacity + rank], tile)
        want_ref[owner] = tile


def wanted(table, length, devices, pages_dev, page_size):
    capacity = pages_dev // devices
    return pl.pallas_call(
        functools.partial(want_kernel, pages_dev, capacity, page_size),
        out_shape=(
            jax.ShapeDtypeStruct((devices, 8, 128), jnp.int32),
            jax.ShapeDtypeStruct((devices * capacity,), jnp.int32),
        ),
        in_specs=[SMEM, SMEM],
        out_specs=(VMEM, SMEM),
        scratch_shapes=[
            pltpu.SMEM((devices * capacity,), jnp.int32),
            pltpu.SMEM((devices,), jnp.int32),
        ],
        name="wanted",
    )(table, length)


def gather_kernel(capacity, asked_hbm, pages_ref, out_ref, own_ref, asked, held, sem, sems_in, sems_out):
    me = lax.axis_index("req")
    load = pltpu.make_async_copy(asked_hbm.at[:, 0:1, :], asked, sem.at[0])
    load.start()
    load.wait()
    count = held.shape[0]
    reads = []
    for index in range(count):
        slot = asked[index // capacity, 0, index % capacity]
        reads.append(
            pltpu.make_async_copy(pages_ref.at[slot], held.at[index], sems_in.at[index])
        )
        reads[-1].start()
    writes = []
    for index in range(count):
        reads[index].wait()
        writes.append(
            pltpu.make_async_copy(held.at[index], out_ref.at[index], sems_out.at[index])
        )
        writes[-1].start()
    mine = pltpu.make_async_copy(held.at[pl.ds(me * capacity, capacity)], own_ref, sem.at[1])
    mine.start()
    for write in writes:
        write.wait()
    mine.wait()


def gather_pages(asked, kv_pages, capacity):
    count = asked.shape[0] * capacity
    page = kv_pages.shape[1:]
    return pl.pallas_call(
        functools.partial(gather_kernel, capacity),
        out_shape=(
            jax.ShapeDtypeStruct((count,) + page, kv_pages.dtype),
            jax.ShapeDtypeStruct((capacity,) + page, kv_pages.dtype),
        ),
        in_specs=[HBM, HBM],
        out_specs=(HBM, HBM),
        scratch_shapes=[
            pltpu.SMEM((asked.shape[0], 1, asked.shape[2]), jnp.int32),
            pltpu.VMEM((count,) + page, kv_pages.dtype),
            pltpu.SemaphoreType.DMA((2,)),
            pltpu.SemaphoreType.DMA((count,)),
            pltpu.SemaphoreType.DMA((count,)),
        ],
        compiler_params=params(60),
        cost_estimate=LIGHT,
        name="gather_pages",
    )(asked, kv_pages)


def silu(value):
    return value / (1.0 + jnp.exp(-value))


def front_kernel(
    core_ref, mine_ref, other_ref, gain_ref, cos_ref, sin_ref,
    histx_ref, histbc_ref, convx_ref, convbc_ref, bias_ref, rate_ref, skip_ref, mixer_gain_ref,
    wdt_hbm, wbc_hbm, wx_hbm, wz_hbm, wq_hbm, wk_hbm, wv_hbm, state_hbm,
    q_ref, k_ref, v_ref, gated_ref, square_ref, last_hbm,
    normed, wdt, wbc, wx, wz, wq, wkv, state_ref, last_ref, sems,
    x_ref, z_ref, bc_ref, padded, inner, cum, cum_t, step_size, b_ref, c_ref,
):
    copies = [
        pltpu.make_async_copy(source, target, sems.at[i])
        for i, (source, target) in enumerate(
            (
                (wdt_hbm, wdt),
                (wbc_hbm, wbc),
                (wx_hbm, wx),
                (wz_hbm, wz),
                (state_hbm, state_ref),
                (wq_hbm, wq),
                (wk_hbm, wkv.at[:, 0:HEAD_SIZE]),
                (wv_hbm, wkv.at[:, HEAD_SIZE : 2 * HEAD_SIZE]),
            )
        )
    ]
    for copy in copies:
        copy.start()

    rows, half = mine_ref.shape
    core = core_ref[0]
    here = pl.ds(pl.multiple_of(core * half, half), half)
    there = pl.ds(pl.multiple_of((1 - core) * half, half), half)
    step = 64

    def norm_rows(i, carry):
        block = pl.ds(pl.multiple_of(i * step, step), step)
        mine = mine_ref[block, :].astype(F32)
        other = other_ref[block, :].astype(F32)
        total = jnp.sum(mine * mine + other * other, axis=-1, keepdims=True)
        scale = lax.rsqrt(total / (2 * half) + EPSILON)
        normed[block, here] = (mine * scale * gain_ref[:, here]).astype(BF16)
        normed[block, there] = (other * scale * gain_ref[:, there]).astype(BF16)
        return carry

    lax.fori_loop(0, rows // step, norm_rows, 0)

    def dense(weight, target):
        for start in range(0, weight.shape[1], 256):
            tile = slice(start, start + 256)
            target[:, tile] = jnp.dot(
                normed[...], weight[:, tile], preferred_element_type=F32
            ).astype(BF16)

    copies[0].wait()
    raw = lax.dot_general(
        normed[...], wdt[...], (((1,), (1,)), ((), ())), preferred_element_type=F32
    ) + bias_ref[...]
    heads = raw.shape[1]
    copies[1].wait()
    dense(wbc, bc_ref)
    copies[2].wait()
    dense(wx, x_ref)
    copies[3].wait()
    dense(wz, z_ref)

    taps = convx_ref.shape[0]
    group = 2 * MP
    middle = rows // 2

    def conv(history, fresh, kernel):
        width = fresh.shape[1]
        padded[0:8, 0:width] = jnp.zeros((8, width), F32)
        padded[8 - (taps - 1) : 8, 0:width] = history.astype(F32)
        padded[8 : 8 + rows, 0:width] = fresh.astype(F32)
        summed = padded[9 - taps : 9 - taps + rows, 0:width] * kernel[0:1, :]
        for tap in range(1, taps):
            begin = 9 - taps + tap
            summed = summed + padded[begin : begin + rows, 0:width] * kernel[tap : tap + 1, :]
        return silu(summed).astype(BF16)

    for start in range(0, 2 * MN, group):
        part = conv(
            histbc_ref[0, :, start : start + group],
            bc_ref[:, start : start + group],
            convbc_ref[:, start : start + group],
        )
        if start < MN:
            b_ref[:, start : start + group] = part
        else:
            c_ref[:, start - MN : start - MN + group] = part

    size = jnp.maximum(raw, 0.0) + jnp.log1p(jnp.exp(-jnp.abs(raw)))
    step_size[:, 0:heads] = size
    row_index = lax.broadcasted_iota(jnp.int32, (rows, rows), 0)
    column_index = lax.broadcasted_iota(jnp.int32, (rows, rows), 1)
    causal = column_index <= row_index
    cum[...] = jnp.zeros((rows, 128), F32)
    cum[:, 0:heads] = -size * (rate_ref[...] * LOG2E)
    cum[...] = jnp.dot(
        causal.astype(F32), cum[...], precision=lax.Precision.HIGHEST, preferred_element_type=F32
    )
    cum_t[...] = cum[...].T
    inner[...] = jnp.where(
        causal,
        lax.dot_general(c_ref[...], b_ref[...], CONTRACT_LAST, preferred_element_type=F32),
        0.0,
    )
    copies[4].wait()
    first = lax.broadcasted_iota(jnp.int32, (1, group), 1) < MP
    first_rows = lax.broadcasted_iota(jnp.int32, (group, 1), 0) < MP
    squares = jnp.zeros((rows, group), F32)
    for pair in range(heads // 2):
        cols = slice(pair * group, (pair + 1) * group)
        one, two = 2 * pair, 2 * pair + 1
        x_rows = conv(histx_ref[0, :, cols], x_ref[:, cols], convx_ref[:, cols]).astype(F32)
        sizes = jnp.where(first, step_size[:, one : one + 1], step_size[:, two : two + 1])
        fades = jnp.where(first, cum[:, one : one + 1], cum[:, two : two + 1])
        last_fade = fades[rows - 1 : rows, :]
        moved_float = x_rows * sizes
        moved = moved_float.astype(BF16)
        tail_moved = moved_float * jnp.exp2(last_fade - fades)
        state = state_ref[cols, :]
        state_high = state.astype(BF16)
        state_low = (state - state_high.astype(F32)).astype(BF16)
        carried = lax.dot_general(
            c_ref[...], state_high, CONTRACT_LAST, preferred_element_type=F32
        ) + lax.dot_general(c_ref[...], state_low, CONTRACT_LAST, preferred_element_type=F32)
        blocks = []
        for begin in (0, middle):
            end = begin + middle
            sides = []
            for head in (one, two):
                gap = cum[begin:end, head : head + 1] - cum_t[head : head + 1, 0:end]
                mixing = (jnp.exp2(jnp.minimum(gap, 0.0)) * inner[begin:end, 0:end]).astype(BF16)
                sides.append(jnp.dot(mixing, moved[0:end, :], preferred_element_type=F32))
            blocks.append(jnp.where(first, sides[0], sides[1]))
        ssm_y = (
            jnp.concatenate(blocks, axis=0)
            + carried * jnp.exp2(fades)
            + jnp.where(first, skip_ref[one], skip_ref[two]) * x_rows
        )
        gated = ssm_y * silu(z_ref[:, cols].astype(F32))
        squares = squares + gated * gated
        gated_ref[:, cols] = (gated * mixer_gain_ref[:, cols]).astype(BF16)
        added = jnp.dot(tail_moved.T.astype(BF16), b_ref[...], preferred_element_type=F32)
        ends = jnp.exp2(cum_t[one : two + 1, rows - 1 : rows])
        keep = jnp.where(first_rows, ends[0:1, :], ends[1:2, :])
        last_ref[cols, :] = keep * state + added
    square_ref[...] = jnp.sum(squares.T, axis=0, keepdims=True)
    give_back = pltpu.make_async_copy(last_ref, last_hbm, sems.at[8])
    give_back.start()

    def rope(vectors):
        return vectors * cos_ref[...] + pltpu.roll(vectors, HEAD_SIZE // 2, 1) * sin_ref[...]

    copies[5].wait()
    for tile in range(wq.shape[1] // 256):
        two_heads = jnp.dot(
            normed[...], wq[:, tile * 256 : tile * 256 + 256], preferred_element_type=F32
        )
        for side in range(2):
            head = 2 * tile + side
            q_ref[head * rows : (head + 1) * rows, :] = rope(
                two_heads[:, side * HEAD_SIZE : (side + 1) * HEAD_SIZE]
            ).astype(BF16)
    copies[6].wait()
    copies[7].wait()
    key_value = jnp.dot(normed[...], wkv[...], preferred_element_type=F32)
    k_ref[...] = rope(key_value[:, :HEAD_SIZE]).astype(BF16)
    v_ref[...] = key_value[:, HEAD_SIZE:].astype(BF16)
    give_back.wait()


def front(
    core, mine, other, gain, cosine, sine,
    histx, histbc, convx, convbc, bias, rate, skip, mixer_gain,
    wdt, wbc, wx, wz, wq, wk, wv, state,
):
    rows, half = mine.shape
    width = 2 * half

    def out(shape, dtype=BF16):
        return jax.ShapeDtypeStruct(shape, dtype)

    return pl.pallas_call(
        front_kernel,
        out_shape=(
            out((wq.shape[1] // HEAD_SIZE * rows, HEAD_SIZE)),
            out((rows, wk.shape[1])),
            out((rows, wv.shape[1])),
            out((rows, wx.shape[1])),
            out((1, rows), F32),
            out(state.shape, F32),
        ),
        in_specs=[SMEM] + [VMEM] * 11 + [SMEM, VMEM] + [HBM] * 8,
        out_specs=(VMEM,) * 5 + (HBM,),
        scratch_shapes=[
            pltpu.VMEM((rows, width), BF16),
            pltpu.VMEM(wdt.shape, BF16),
            pltpu.VMEM(wbc.shape, BF16),
            pltpu.VMEM(wx.shape, BF16),
            pltpu.VMEM(wz.shape, BF16),
            pltpu.VMEM(wq.shape, BF16),
            pltpu.VMEM((width, 2 * HEAD_SIZE), BF16),
            pltpu.VMEM(state.shape, F32),
            pltpu.VMEM(state.shape, F32),
            pltpu.SemaphoreType.DMA((9,)),
            pltpu.VMEM((rows, wx.shape[1]), BF16),
            pltpu.VMEM((rows, wz.shape[1]), BF16),
            pltpu.VMEM((rows, wbc.shape[1]), BF16),
            pltpu.VMEM((rows + 8, 2 * MP), F32),
            pltpu.VMEM((rows, rows), F32),
            pltpu.VMEM((rows, 128), F32),
            pltpu.VMEM((128, rows), F32),
            pltpu.VMEM((rows, 128), F32),
            pltpu.VMEM((rows, MN), BF16),
            pltpu.VMEM((rows, MN), BF16),
        ],
        compiler_params=params(60),
        cost_estimate=LIGHT,
        name="front",
    )(
        core, mine, other, gain, cosine, sine,
        histx, histbc, convx, convbc, bias, rate, skip, mixer_gain,
        wdt, wbc, wx, wz, wq, wk, wv, state,
    )


CONTRACT_LAST = (((1,), (1,)), ((), ()))
CHUNK = 512


def across(column, width):
    return jnp.concatenate([column] * (width // HEAD_SIZE), axis=1)


def softmax_step(scores, values, state):
    count = scores.shape[1]
    top = jnp.broadcast_to(jnp.max(scores, axis=-1, keepdims=True), (scores.shape[0], HEAD_SIZE))
    if state is not None:
        top = jnp.maximum(state[2], top)
    weights = jnp.exp2((scores - across(top, count)) * SCORE_SCALE).astype(BF16)
    values = jnp.concatenate([values, jnp.ones((count, HEAD_SIZE), BF16)], axis=1)
    added = jnp.dot(weights, values, preferred_element_type=F32)
    summed, total = added[:, :HEAD_SIZE], added[:, HEAD_SIZE:]
    if state is not None:
        fade = jnp.exp2((state[2] - top) * SCORE_SCALE)
        summed, total = state[0] * fade + summed, state[1] * fade + total
    return summed, total, top


def page_step(query, keys, values, seen, state):
    pages, tokens, width = keys.shape
    scores = lax.dot_general(
        query, keys.reshape(pages * tokens, width), CONTRACT_LAST, preferred_element_type=F32
    )
    token = lax.broadcasted_iota(jnp.int32, (1, tokens), 1)
    hide = jnp.concatenate(
        [jnp.where(token >= seen[page], NEG_FILL, 0.0) for page in range(pages)], axis=1
    )
    return softmax_step(scores + hide, values.reshape(pages * tokens, width), state)


def attend_early_kernel(masks, picks, fresh, seen_ref, q_hbm, *refs):
    count = max(array for array, _ in picks) + 1
    given = 2 if fresh else 3
    start_hbm, arrays = refs[:given], refs[given : given + count]
    outs = refs[given + count : given + count + 3]
    q_ref, k_ref, v_ref, kv_ref, states, sems, sems_out = refs[given + count + 3 :]
    rows = k_ref.shape[0]
    pages, _, tokens, _ = kv_ref.shape
    capacity = pages // len(masks)
    me = lax.axis_index("req")
    targets = (k_ref, v_ref) if fresh else (states.at[0], states.at[1], states.at[2])
    copies = [pltpu.make_async_copy(q_hbm, q_ref, sems.at[0])]
    for index, (source, target) in enumerate(zip(start_hbm, targets)):
        copies.append(pltpu.make_async_copy(source, target, sems.at[1 + index]))
    for index, (array, entry) in enumerate(picks):
        source = arrays[array] if entry is None else arrays[array].at[entry]
        copies.append(
            pltpu.make_async_copy(
                source, kv_ref.at[pl.ds(index * capacity, capacity)], sems.at[4 + index]
            )
        )
    for copy in copies:
        copy.start()
    seen = [seen_ref[(me ^ mask) * capacity + rank] for mask in masks for rank in range(capacity)]
    row = lax.broadcasted_iota(jnp.int32, (rows, rows), 0)
    column = lax.broadcasted_iota(jnp.int32, (rows, rows), 1)
    for copy in copies:
        copy.wait()
    per_chunk = CHUNK // tokens
    sends = []
    for head, start in enumerate(range(0, q_ref.shape[0], rows)):
        here = slice(start, start + rows)
        if fresh:
            scores = lax.dot_general(
                q_ref[here, :], k_ref[...], CONTRACT_LAST, preferred_element_type=F32
            )
            state = softmax_step(jnp.where(column <= row, scores, NEG_FILL), v_ref[...], None)
        else:
            state = (states[0, here, :], states[1, here, :], states[2, here, :])
        for begin in range(0, pages, per_chunk):
            span = slice(begin, begin + per_chunk)
            state = page_step(q_ref[here, :], kv_ref[span, 0], kv_ref[span, 1], seen[span], state)
        for kind in range(3):
            states[kind, here, :] = state[kind]
            send = pltpu.make_async_copy(
                states.at[kind, here, :], outs[kind].at[here, :], sems_out.at[3 * head + kind]
            )
            send.start()
            sends.append(send)
    for send in sends:
        send.wait()


def attend_early(seen, queries, start, rows, arrays, masks, picks):
    count = queries.shape[0]
    block = arrays[0].shape[-4:]
    pages = len(masks) * block[0]
    fresh = len(start) == 2
    return pl.pallas_call(
        functools.partial(attend_early_kernel, masks, picks, fresh),
        out_shape=(jax.ShapeDtypeStruct((count, HEAD_SIZE), F32),) * 3,
        in_specs=[SMEM] + [HBM] * (1 + len(start) + len(arrays)),
        out_specs=(HBM,) * 3,
        scratch_shapes=[
            pltpu.VMEM(queries.shape, BF16),
            pltpu.VMEM((rows, HEAD_SIZE), BF16),
            pltpu.VMEM((rows, HEAD_SIZE), BF16),
            pltpu.VMEM((pages,) + block[1:], BF16),
            pltpu.VMEM((3, count, HEAD_SIZE), F32),
            pltpu.SemaphoreType.DMA((4 + len(masks),)),
            pltpu.SemaphoreType.DMA((3 * count // rows,)),
        ],
        compiler_params=params(60),
        cost_estimate=LIGHT,
        name="attend_first" if fresh else "attend_more",
    )(seen, queries, *start, *arrays)


def attend_late_kernel(
    masks, core_ref, seen_ref, q_hbm, sum_hbm, total_hbm, top_hbm, weight_hbm, part_hbm, kv_hbm,
    context_ref, out_ref, q_ref, near, far, kv_ref, weight_ref, part_ref, sems, sems_late,
):
    pages, _, tokens, _ = kv_ref.shape
    capacity = pages // len(masks)
    me = lax.axis_index("req")
    rows, half = out_ref.shape
    heads = q_ref.shape[0] // rows
    per_chunk = CHUNK // tokens
    pages_in = [
        pltpu.make_async_copy(
            kv_hbm.at[pl.ds((me ^ mask) * capacity, capacity)],
            kv_ref.at[pl.ds(index * capacity, capacity)],
            sems.at[1 + index],
        )
        for index, mask in enumerate(masks)
    ]
    queries_in = pltpu.make_async_copy(q_hbm, q_ref, sems.at[0])
    there = pl.ds(pl.multiple_of((1 - core_ref[0]) * half, half), half)
    late = [
        pltpu.make_async_copy(source, near.at[kind], sems_late.at[kind])
        for kind, source in enumerate((sum_hbm, total_hbm, top_hbm))
    ] + [
        pltpu.make_async_copy(weight_hbm.at[:, there], weight_ref, sems_late.at[3]),
        pltpu.make_async_copy(part_hbm, part_ref, sems_late.at[4]),
    ]
    seen = [seen_ref[(me ^ mask) * capacity + rank] for mask in masks for rank in range(capacity)]
    ahead = max(2 * per_chunk // capacity, 1)
    split = ahead * capacity
    queries_in.start()
    for copy in pages_in:
        copy.start()
    queries_in.wait()
    for copy in pages_in[:ahead]:
        copy.wait()
    for first in (True, False):
        if not first:
            for copy in pages_in[ahead:]:
                copy.wait()
            for copy in late:
                copy.start()
        for head in range(heads):
            here = slice(head * rows, (head + 1) * rows)
            state = None if first else (far[0, here, :], far[1, here, :], far[2, here, :])
            for begin in range(*((0, split) if first else (split, pages)), per_chunk):
                span = slice(begin, min(begin + per_chunk, split if first else pages))
                state = page_step(
                    q_ref[here, :], kv_ref[span, 0], kv_ref[span, 1], seen[span], state
                )
            for kind in range(3):
                far[kind, here, :] = state[kind]
    for copy in late:
        copy.wait()
    for head in range(heads):
        here = slice(head * rows, (head + 1) * rows)
        top = jnp.maximum(near[2, here, :], far[2, here, :])
        fade_near = jnp.exp2((near[2, here, :] - top) * SCORE_SCALE)
        fade_far = jnp.exp2((far[2, here, :] - top) * SCORE_SCALE)
        summed = near[0, here, :] * fade_near + far[0, here, :] * fade_far
        total = near[1, here, :] * fade_near + far[1, here, :] * fade_far
        context_ref[:, head * HEAD_SIZE : (head + 1) * HEAD_SIZE] = (summed / total).astype(BF16)
    for start in range(0, half, 256):
        tile = slice(start, start + 256)
        out_ref[:, tile] = (
            jnp.dot(context_ref[...], weight_ref[:, tile], preferred_element_type=F32)
            + part_ref[:, tile]
        ).astype(BF16)


def attend_late(core, seen, queries, state, weight, part, kv, masks):
    rows, half = part.shape
    count = queries.shape[0]
    pages = len(masks) * kv.shape[0] // lax.axis_size("req")
    return pl.pallas_call(
        functools.partial(attend_late_kernel, masks),
        out_shape=(
            jax.ShapeDtypeStruct((rows, count // rows * HEAD_SIZE), BF16),
            jax.ShapeDtypeStruct((rows, half), BF16),
        ),
        in_specs=[SMEM] * 2 + [HBM] * 7,
        out_specs=(VMEM, VMEM),
        scratch_shapes=[
            pltpu.VMEM(queries.shape, BF16),
            pltpu.VMEM((3, count, HEAD_SIZE), F32),
            pltpu.VMEM((3, count, HEAD_SIZE), F32),
            pltpu.VMEM((pages,) + kv.shape[1:], BF16),
            pltpu.VMEM((weight.shape[0], half), BF16),
            pltpu.VMEM((rows, half), F32),
            pltpu.SemaphoreType.DMA((1 + len(masks),)),
            pltpu.SemaphoreType.DMA((5,)),
        ],
        compiler_params=params(60),
        cost_estimate=LIGHT,
        name="attend_late",
    )(core, seen, queries, *state, weight, part, kv)


def mixer_out_kernel(
    core_ref, gated_ref, scale_ref, weight_ref, attn_hbm, theirs_ref, ours_ref, attn_ref, sem
):
    half = ours_ref.shape[1]
    mine = pl.ds(pl.multiple_of(core_ref[0] * half, half), half)
    cut = pltpu.make_async_copy(attn_hbm.at[:, mine], attn_ref, sem.at[0])
    cut.start()
    for start in range(0, half, 256):
        for core, out_ref in ((1 - core_ref[0], theirs_ref), (core_ref[0], ours_ref)):
            here = pl.ds(pl.multiple_of(core * half + start, 256), 256)
            out_ref[:, start : start + 256] = (
                jnp.dot(gated_ref[...], weight_ref[:, here], preferred_element_type=F32)
                * scale_ref[...]
            )
    cut.wait()


def mixer_out(core, gated, scale, weight, attn_weight):
    rows, depth = gated.shape
    width = weight.shape[1]
    return pl.pallas_call(
        mixer_out_kernel,
        out_shape=(jax.ShapeDtypeStruct((rows, width // 2), F32),) * 2
        + (jax.ShapeDtypeStruct((attn_weight.shape[0], width // 2), BF16),),
        in_specs=[SMEM] + [VMEM] * 3 + [HBM],
        out_specs=(VMEM,) * 3,
        scratch_shapes=[pltpu.SemaphoreType.DMA((1,))],
        compiler_params=params(16),
        cost_estimate=LIGHT,
        name="mixer_out",
    )(core, gated, scale, weight, attn_weight)


def ours_kernel(context_ref, weight_ref, part_ref, out_ref):
    for start in range(0, out_ref.shape[1], 256):
        tile = slice(start, start + 256)
        out_ref[:, tile] = (
            jnp.dot(context_ref[...], weight_ref[:, tile], preferred_element_type=F32)
            + part_ref[:, tile]
        ).astype(BF16)


def ours_half(context, weight, part):
    return pl.pallas_call(
        ours_kernel,
        out_shape=jax.ShapeDtypeStruct(part.shape, BF16),
        in_specs=[VMEM] * 3,
        out_specs=VMEM,
        compiler_params=params(16),
        cost_estimate=LIGHT,
        name="ours_half",
    )(context, weight, part)


def shards(
    tokens,
    attn_gain,
    w_query,
    key_weight,
    value_weight,
    w_attn_out,
    kv_pages,
    page_table,
    cached_len,
    w_gate_z,
    w_ssm_in,
    w_bc,
    w_dt,
    conv_w_x,
    conv_w_bc,
    conv_x_state,
    conv_bc_state,
    dt_bias,
    decay_rate,
    skip_gain,
    mixer_gain,
    w_mixer_out,
    ssm_state,
):
    swap = [(0, 1), (1, 0)]
    core = lax.axis_index("tp").astype(jnp.int32).reshape(1)
    row_count = tokens.shape[0]
    devices = lax.axis_size("req")
    pages_dev = kv_pages.shape[0]
    capacity = pages_dev // devices
    page_size = kv_pages.shape[3]
    length = cached_len[0]

    want, seen = wanted(page_table, cached_len, devices, pages_dev, page_size)
    cosine, sine = rope_tables(length + jnp.arange(row_count, dtype=jnp.int32))
    other = lax.ppermute(tokens, "tp", swap)

    def exchange(blocks):
        return lax.all_to_all(blocks, "req", split_axis=0, concat_axis=0, tiled=True)

    fetched, own = gather_pages(
        exchange(want), kv_pages.reshape((pages_dev, 2, page_size, HEAD_SIZE)), capacity
    )
    arrived = exchange(fetched.reshape((devices, capacity) + fetched.shape[1:])).reshape(
        fetched.shape
    )

    heads = w_dt.shape[1]
    queries, fresh_keys, fresh_values, gated, squares, last_state = front(
        core, tokens, other, attn_gain[None, :], cosine, sine,
        conv_x_state, conv_bc_state, conv_w_x, conv_w_bc,
        dt_bias[None, :], decay_rate[None, :], skip_gain,
        mixer_gain[None, :],
        w_dt.T, w_bc, w_ssm_in, w_gate_z, w_query, key_weight, value_weight,
        ssm_state.reshape((heads * MP, MN)),
    )
    total = squares + lax.ppermute(squares, "tp", swap)
    scale = lax.rsqrt(total.reshape((row_count, 1)) / DSSM + EPSILON)
    part_theirs, part_ours, weight_ours = mixer_out(core, gated, scale, w_mixer_out, w_attn_out)
    state = attend_early(
        seen, queries, (fresh_keys, fresh_values), row_count, [own], [0], [(0, None)]
    )
    context, theirs = attend_late(
        core, seen, queries, state, w_attn_out, part_theirs, arrived, list(range(1, devices))
    )
    received = lax.ppermute(theirs, "tp", swap)
    ours = ours_half(context, weight_ours, part_ours)
    mixed = (ours.astype(F32) + received.astype(F32)).astype(BF16)
    return (mixed, last_state.reshape(ssm_state.shape))


def solution(mesh):
    return jax.shard_map(
        shards,
        mesh=mesh,
        in_specs=(
            P("req", "tp"),
            P(),
            P(None, "tp"),
            P(None, "tp"),
            P(None, "tp"),
            P("tp", None),
            P("req", None, "tp", None, None),
            P("req", None),
            P("req"),
            P(None, "tp"),
            P(None, "tp"),
            P(),
            P(None, "tp"),
            P(None, "tp"),
            P(),
            P("req", None, "tp"),
            P("req", None, None),
            P("tp"),
            P("tp"),
            P("tp"),
            P("tp"),
            P("tp", None),
            P("req", "tp", None, None),
        ),
        out_specs=(P("req", "tp"), P("req", "tp", None, None)),
        check_vma=False,
    )
```

```python
import functools

import jax
import jax.numpy as jnp
from jax import lax
from jax.experimental import pallas as pl
from jax.experimental.pallas import tpu as pltpu
from jax.sharding import PartitionSpec as P

HEAD_SIZE = 128
MP = 64
MN = 256
DSSM = 1536

EPSILON = 1e-05
ROPE_BASE = 100000.0
NEG_FILL = -1e30
LOG2E = 1.4426950408889634
SCORE_SCALE = HEAD_SIZE ** (-0.5) * LOG2E

VMEM = pl.BlockSpec(memory_space=pltpu.VMEM)
SMEM = pl.BlockSpec(memory_space=pltpu.SMEM)
HBM = pl.BlockSpec(memory_space=pltpu.HBM)
F32 = jnp.float32
BF16 = jnp.bfloat16
LIGHT = pl.CostEstimate(flops=10**6, bytes_accessed=10**4, transcendentals=0)


def params(mebibytes):
    return pltpu.CompilerParams(vmem_limit_bytes=mebibytes * 2**20)


def rope_tables(token_positions):
    half_width = HEAD_SIZE // 2
    inverse = ROPE_BASE ** (-2.0 * jnp.arange(half_width, dtype=F32) / HEAD_SIZE)
    angles = token_positions.astype(F32)[:, None] * inverse[None, :]
    cosine, sine = jnp.cos(angles), jnp.sin(angles)
    return (
        jnp.concatenate([cosine, cosine], axis=-1),
        jnp.concatenate([-sine, sine], axis=-1),
    )


def want_kernel(pages_dev, capacity, page_size, table_ref, length_ref, want_ref, seen_ref, slots, counts):
    for i in range(counts.shape[0]):
        counts[i] = 0
    for i in range(slots.shape[0]):
        slots[i] = 0
        seen_ref[i] = 0
    for page in range(table_ref.shape[1]):
        entry = table_ref[0, page]
        owner = entry // pages_dev
        rank = counts[owner]
        counts[owner] = rank + 1
        place = owner * capacity + rank
        slots[place] = entry - owner * pages_dev
        seen_ref[place] = jnp.clip(length_ref[0] - page * page_size, 0, page_size)
    lane = lax.broadcasted_iota(jnp.int32, want_ref.shape[1:], 1)
    for owner in range(want_ref.shape[0]):
        tile = jnp.zeros(want_ref.shape[1:], jnp.int32)
        for rank in range(capacity):
            tile = jnp.where(lane == rank, slots[owner * capacity + rank], tile)
        want_ref[owner] = tile


def wanted(table, length, devices, pages_dev, page_size):
    capacity = pages_dev // devices
    return pl.pallas_call(
        functools.partial(want_kernel, pages_dev, capacity, page_size),
        out_shape=(
            jax.ShapeDtypeStruct((devices, 1, 128), jnp.int32),
            jax.ShapeDtypeStruct((devices * capacity,), jnp.int32),
        ),
        in_specs=[SMEM, SMEM],
        out_specs=(VMEM, SMEM),
        scratch_shapes=[
            pltpu.SMEM((devices * capacity,), jnp.int32),
            pltpu.SMEM((devices,), jnp.int32),
        ],
        name="wanted",
    )(table, length)


def gather_kernel(capacity, asked_hbm, pages_ref, out_ref, own_ref, asked, held, sem, sems_in, sems_out):
    me = lax.axis_index("req")
    load = pltpu.make_async_copy(asked_hbm, asked, sem.at[0])
    load.start()
    load.wait()
    count = held.shape[0]
    reads = []
    for index in range(count):
        slot = asked[index // capacity, 0, index % capacity]
        reads.append(
            pltpu.make_async_copy(pages_ref.at[slot], held.at[index], sems_in.at[index])
        )
        reads[-1].start()
    writes = []
    for request in range(count // capacity):
        block = pl.ds(request * capacity, capacity)
        for read in reads[request * capacity : (request + 1) * capacity]:
            read.wait()
        writes.append(
            pltpu.make_async_copy(held.at[block], out_ref.at[block], sems_out.at[request])
        )
        writes[-1].start()
    mine = pltpu.make_async_copy(held.at[pl.ds(me * capacity, capacity)], own_ref, sem.at[1])
    mine.start()
    for write in writes:
        write.wait()
    mine.wait()


def gather_pages(asked, kv_pages, capacity):
    count = asked.shape[0] * capacity
    page = kv_pages.shape[1:]
    return pl.pallas_call(
        functools.partial(gather_kernel, capacity),
        out_shape=(
            jax.ShapeDtypeStruct((count,) + page, kv_pages.dtype),
            jax.ShapeDtypeStruct((capacity,) + page, kv_pages.dtype),
        ),
        in_specs=[HBM, HBM],
        out_specs=(HBM, HBM),
        scratch_shapes=[
            pltpu.SMEM(asked.shape, jnp.int32),
            pltpu.VMEM((count,) + page, kv_pages.dtype),
            pltpu.SemaphoreType.DMA((2,)),
            pltpu.SemaphoreType.DMA((count,)),
            pltpu.SemaphoreType.DMA((asked.shape[0],)),
        ],
        compiler_params=params(60),
        cost_estimate=LIGHT,
        name="gather_pages",
    )(asked, kv_pages)


def silu(value):
    return value / (1.0 + jnp.exp(-value))


def front_kernel(
    core_ref, mine_ref, other_ref, gain_ref, cos_ref, sin_ref,
    histx_ref, histbc_ref, convx_ref, convbc_ref, bias_ref, rate_ref, skip_ref, mixer_gain_ref,
    wdt_hbm, wbc_hbm, wx_hbm, wz_hbm, wq_hbm, wk_hbm, wv_hbm, state_hbm,
    q_ref, k_ref, v_ref, gated_ref, square_ref, last_hbm,
    normed, wdt, wbc, wx, wz, wq, wkv, state_ref, last_ref, sems,
    x_ref, z_ref, bc_ref, padded, inner, cum, cum_t, step_size, b_ref, c_ref,
):
    copies = [
        pltpu.make_async_copy(source, target, sems.at[i])
        for i, (source, target) in enumerate(
            (
                (wdt_hbm, wdt),
                (wbc_hbm, wbc),
                (wx_hbm, wx),
                (wz_hbm, wz),
                (state_hbm, state_ref),
                (wq_hbm, wq),
                (wk_hbm, wkv.at[:, 0:HEAD_SIZE]),
                (wv_hbm, wkv.at[:, HEAD_SIZE : 2 * HEAD_SIZE]),
            )
        )
    ]
    for copy in copies:
        copy.start()

    rows, half = mine_ref.shape
    core = core_ref[0]
    here = pl.ds(pl.multiple_of(core * half, half), half)
    there = pl.ds(pl.multiple_of((1 - core) * half, half), half)
    step = 64

    def norm_rows(i, carry):
        block = pl.ds(pl.multiple_of(i * step, step), step)
        mine = mine_ref[block, :].astype(F32)
        other = other_ref[block, :].astype(F32)
        total = jnp.sum(mine * mine + other * other, axis=-1, keepdims=True)
        scale = lax.rsqrt(total / (2 * half) + EPSILON)
        normed[block, here] = (mine * scale * gain_ref[:, here]).astype(BF16)
        normed[block, there] = (other * scale * gain_ref[:, there]).astype(BF16)
        return carry

    lax.fori_loop(0, rows // step, norm_rows, 0)

    def dense(weight, target):
        for start in range(0, weight.shape[1], 256):
            tile = slice(start, start + 256)
            target[:, tile] = jnp.dot(
                normed[...], weight[:, tile], preferred_element_type=F32
            ).astype(BF16)

    copies[0].wait()
    raw = lax.dot_general(
        normed[...], wdt[...], (((1,), (1,)), ((), ())), preferred_element_type=F32
    ) + bias_ref[...]
    heads = raw.shape[1]
    copies[1].wait()
    dense(wbc, bc_ref)
    copies[2].wait()
    dense(wx, x_ref)
    copies[3].wait()
    dense(wz, z_ref)

    taps = convx_ref.shape[0]
    group = 2 * MP
    middle = rows // 2

    def conv(history, fresh, kernel):
        width = fresh.shape[1]
        padded[0:8, 0:width] = jnp.zeros((8, width), F32)
        padded[8 - (taps - 1) : 8, 0:width] = history.astype(F32)
        padded[8 : 8 + rows, 0:width] = fresh.astype(F32)
        summed = padded[9 - taps : 9 - taps + rows, 0:width] * kernel[0:1, :]
        for tap in range(1, taps):
            begin = 9 - taps + tap
            summed = summed + padded[begin : begin + rows, 0:width] * kernel[tap : tap + 1, :]
        return silu(summed).astype(BF16)

    for start in range(0, 2 * MN, group):
        part = conv(
            histbc_ref[0, :, start : start + group],
            bc_ref[:, start : start + group],
            convbc_ref[:, start : start + group],
        )
        if start < MN:
            b_ref[:, start : start + group] = part
        else:
            c_ref[:, start - MN : start - MN + group] = part

    size = jnp.maximum(raw, 0.0) + jnp.log1p(jnp.exp(-jnp.abs(raw)))
    step_size[:, 0:heads] = size
    row_index = lax.broadcasted_iota(jnp.int32, (rows, rows), 0)
    column_index = lax.broadcasted_iota(jnp.int32, (rows, rows), 1)
    causal = column_index <= row_index
    cum[...] = jnp.zeros((rows, 128), F32)
    cum[:, 0:heads] = -size * (rate_ref[...] * LOG2E)
    cum[...] = jnp.dot(
        causal.astype(F32), cum[...], precision=lax.Precision.HIGHEST, preferred_element_type=F32
    )
    cum_t[...] = cum[...].T
    inner[...] = jnp.where(
        causal,
        lax.dot_general(c_ref[...], b_ref[...], CONTRACT_LAST, preferred_element_type=F32),
        0.0,
    )
    copies[4].wait()
    first = lax.broadcasted_iota(jnp.int32, (1, group), 1) < MP
    first_rows = lax.broadcasted_iota(jnp.int32, (group, 1), 0) < MP
    squares = jnp.zeros((rows, group), F32)
    for pair in range(heads // 2):
        cols = slice(pair * group, (pair + 1) * group)
        one, two = 2 * pair, 2 * pair + 1
        x_rows = conv(histx_ref[0, :, cols], x_ref[:, cols], convx_ref[:, cols]).astype(F32)
        sizes = jnp.where(first, step_size[:, one : one + 1], step_size[:, two : two + 1])
        fades = jnp.where(first, cum[:, one : one + 1], cum[:, two : two + 1])
        last_fade = fades[rows - 1 : rows, :]
        moved_float = x_rows * sizes
        moved = moved_float.astype(BF16)
        tail_moved = moved_float * jnp.exp2(last_fade - fades)
        state = state_ref[cols, :]
        state_high = state.astype(BF16)
        state_low = (state - state_high.astype(F32)).astype(BF16)
        carried = lax.dot_general(
            c_ref[...], state_high, CONTRACT_LAST, preferred_element_type=F32
        ) + lax.dot_general(c_ref[...], state_low, CONTRACT_LAST, preferred_element_type=F32)
        blocks = []
        for begin in (0, middle):
            end = begin + middle
            sides = []
            for head in (one, two):
                gap = cum[begin:end, head : head + 1] - cum_t[head : head + 1, 0:end]
                mixing = (jnp.exp2(jnp.minimum(gap, 0.0)) * inner[begin:end, 0:end]).astype(BF16)
                sides.append(jnp.dot(mixing, moved[0:end, :], preferred_element_type=F32))
            blocks.append(jnp.where(first, sides[0], sides[1]))
        ssm_y = (
            jnp.concatenate(blocks, axis=0)
            + carried * jnp.exp2(fades)
            + jnp.where(first, skip_ref[one], skip_ref[two]) * x_rows
        )
        gated = ssm_y * silu(z_ref[:, cols].astype(F32))
        squares = squares + gated * gated
        gated_ref[:, cols] = (gated * mixer_gain_ref[:, cols]).astype(BF16)
        added = jnp.dot(tail_moved.T.astype(BF16), b_ref[...], preferred_element_type=F32)
        ends = jnp.exp2(cum_t[one : two + 1, rows - 1 : rows])
        keep = jnp.where(first_rows, ends[0:1, :], ends[1:2, :])
        last_ref[cols, :] = keep * state + added
    square_ref[...] = jnp.sum(squares.T, axis=0, keepdims=True)
    give_back = pltpu.make_async_copy(last_ref, last_hbm, sems.at[8])
    give_back.start()

    def rope(vectors):
        return vectors * cos_ref[...] + pltpu.roll(vectors, HEAD_SIZE // 2, 1) * sin_ref[...]

    copies[5].wait()
    for tile in range(wq.shape[1] // 256):
        two_heads = jnp.dot(
            normed[...], wq[:, tile * 256 : tile * 256 + 256], preferred_element_type=F32
        )
        for side in range(2):
            head = 2 * tile + side
            q_ref[head * rows : (head + 1) * rows, :] = rope(
                two_heads[:, side * HEAD_SIZE : (side + 1) * HEAD_SIZE]
            ).astype(BF16)
    copies[6].wait()
    copies[7].wait()
    key_value = jnp.dot(normed[...], wkv[...], preferred_element_type=F32)
    k_ref[...] = rope(key_value[:, :HEAD_SIZE]).astype(BF16)
    v_ref[...] = key_value[:, HEAD_SIZE:].astype(BF16)
    give_back.wait()


def front(
    core, mine, other, gain, cosine, sine,
    histx, histbc, convx, convbc, bias, rate, skip, mixer_gain,
    wdt, wbc, wx, wz, wq, wk, wv, state,
):
    rows, half = mine.shape
    width = 2 * half

    def out(shape, dtype=BF16):
        return jax.ShapeDtypeStruct(shape, dtype)

    return pl.pallas_call(
        front_kernel,
        out_shape=(
            out((wq.shape[1] // HEAD_SIZE * rows, HEAD_SIZE)),
            out((rows, wk.shape[1])),
            out((rows, wv.shape[1])),
            out((rows, wx.shape[1])),
            out((1, rows), F32),
            out(state.shape, F32),
        ),
        in_specs=[SMEM] + [VMEM] * 11 + [SMEM, VMEM] + [HBM] * 8,
        out_specs=(VMEM,) * 5 + (HBM,),
        scratch_shapes=[
            pltpu.VMEM((rows, width), BF16),
            pltpu.VMEM(wdt.shape, BF16),
            pltpu.VMEM(wbc.shape, BF16),
            pltpu.VMEM(wx.shape, BF16),
            pltpu.VMEM(wz.shape, BF16),
            pltpu.VMEM(wq.shape, BF16),
            pltpu.VMEM((width, 2 * HEAD_SIZE), BF16),
            pltpu.VMEM(state.shape, F32),
            pltpu.VMEM(state.shape, F32),
            pltpu.SemaphoreType.DMA((9,)),
            pltpu.VMEM((rows, wx.shape[1]), BF16),
            pltpu.VMEM((rows, wz.shape[1]), BF16),
            pltpu.VMEM((rows, wbc.shape[1]), BF16),
            pltpu.VMEM((rows + 8, 2 * MP), F32),
            pltpu.VMEM((rows, rows), F32),
            pltpu.VMEM((rows, 128), F32),
            pltpu.VMEM((128, rows), F32),
            pltpu.VMEM((rows, 128), F32),
            pltpu.VMEM((rows, MN), BF16),
            pltpu.VMEM((rows, MN), BF16),
        ],
        compiler_params=params(60),
        cost_estimate=LIGHT,
        name="front",
    )(
        core, mine, other, gain, cosine, sine,
        histx, histbc, convx, convbc, bias, rate, skip, mixer_gain,
        wdt, wbc, wx, wz, wq, wk, wv, state,
    )


CONTRACT_LAST = (((1,), (1,)), ((), ()))
CHUNK = 512


def across(column, width):
    return jnp.concatenate([column] * (width // HEAD_SIZE), axis=1)


def softmax_step(scores, values, state):
    count = scores.shape[1]
    top = jnp.broadcast_to(jnp.max(scores, axis=-1, keepdims=True), (scores.shape[0], HEAD_SIZE))
    if state is not None:
        top = jnp.maximum(state[2], top)
    weights = jnp.exp2((scores - across(top, count)) * SCORE_SCALE).astype(BF16)
    values = jnp.concatenate([values, jnp.ones((count, HEAD_SIZE), BF16)], axis=1)
    added = jnp.dot(weights, values, preferred_element_type=F32)
    summed, total = added[:, :HEAD_SIZE], added[:, HEAD_SIZE:]
    if state is not None:
        fade = jnp.exp2((state[2] - top) * SCORE_SCALE)
        summed, total = state[0] * fade + summed, state[1] * fade + total
    return summed, total, top


def page_step(query, keys, values, seen, state):
    pages, tokens, width = keys.shape
    scores = lax.dot_general(
        query, keys.reshape(pages * tokens, width), CONTRACT_LAST, preferred_element_type=F32
    )
    token = lax.broadcasted_iota(jnp.int32, (1, tokens), 1)
    hide = jnp.concatenate(
        [jnp.where(token >= seen[page], NEG_FILL, 0.0) for page in range(pages)], axis=1
    )
    return softmax_step(scores + hide, values.reshape(pages * tokens, width), state)


def attend_early_kernel(masks, picks, fresh, seen_ref, q_hbm, *refs):
    count = max(array for array, _ in picks) + 1
    given = 2 if fresh else 3
    start_hbm, arrays = refs[:given], refs[given : given + count]
    outs = refs[given + count : given + count + 3]
    q_ref, k_ref, v_ref, kv_ref, states, sems, sems_out = refs[given + count + 3 :]
    rows = k_ref.shape[0]
    pages, _, tokens, _ = kv_ref.shape
    capacity = pages // len(masks)
    me = lax.axis_index("req")
    targets = (k_ref, v_ref) if fresh else (states.at[0], states.at[1], states.at[2])
    copies = [pltpu.make_async_copy(q_hbm, q_ref, sems.at[0])]
    for index, (source, target) in enumerate(zip(start_hbm, targets)):
        copies.append(pltpu.make_async_copy(source, target, sems.at[1 + index]))
    for index, (array, entry) in enumerate(picks):
        source = arrays[array] if entry is None else arrays[array].at[entry]
        copies.append(
            pltpu.make_async_copy(
                source, kv_ref.at[pl.ds(index * capacity, capacity)], sems.at[4 + index]
            )
        )
    for copy in copies:
        copy.start()
    seen = [seen_ref[(me ^ mask) * capacity + rank] for mask in masks for rank in range(capacity)]
    row = lax.broadcasted_iota(jnp.int32, (rows, rows), 0)
    column = lax.broadcasted_iota(jnp.int32, (rows, rows), 1)
    for copy in copies:
        copy.wait()
    per_chunk = CHUNK // tokens
    sends = []
    for head, start in enumerate(range(0, q_ref.shape[0], rows)):
        here = slice(start, start + rows)
        if fresh:
            scores = lax.dot_general(
                q_ref[here, :], k_ref[...], CONTRACT_LAST, preferred_element_type=F32
            )
            state = softmax_step(jnp.where(column <= row, scores, NEG_FILL), v_ref[...], None)
        else:
            state = (states[0, here, :], states[1, here, :], states[2, here, :])
        for begin in range(0, pages, per_chunk):
            span = slice(begin, begin + per_chunk)
            state = page_step(q_ref[here, :], kv_ref[span, 0], kv_ref[span, 1], seen[span], state)
        for kind in range(3):
            states[kind, here, :] = state[kind]
            send = pltpu.make_async_copy(
                states.at[kind, here, :], outs[kind].at[here, :], sems_out.at[3 * head + kind]
            )
            send.start()
            sends.append(send)
    for send in sends:
        send.wait()


def attend_early(seen, queries, start, rows, arrays, masks, picks):
    count = queries.shape[0]
    block = arrays[0].shape[-4:]
    pages = len(masks) * block[0]
    fresh = len(start) == 2
    return pl.pallas_call(
        functools.partial(attend_early_kernel, masks, picks, fresh),
        out_shape=(jax.ShapeDtypeStruct((count, HEAD_SIZE), F32),) * 3,
        in_specs=[SMEM] + [HBM] * (1 + len(start) + len(arrays)),
        out_specs=(HBM,) * 3,
        scratch_shapes=[
            pltpu.VMEM(queries.shape, BF16),
            pltpu.VMEM((rows, HEAD_SIZE), BF16),
            pltpu.VMEM((rows, HEAD_SIZE), BF16),
            pltpu.VMEM((pages,) + block[1:], BF16),
            pltpu.VMEM((3, count, HEAD_SIZE), F32),
            pltpu.SemaphoreType.DMA((4 + len(masks),)),
            pltpu.SemaphoreType.DMA((3 * count // rows,)),
        ],
        compiler_params=params(60),
        cost_estimate=LIGHT,
        name="attend_first" if fresh else "attend_more",
    )(seen, queries, *start, *arrays)


def attend_late_kernel(
    masks, seen_ref, q_hbm, sum_hbm, total_hbm, top_hbm, weight_hbm, part_hbm, kv_hbm,
    context_ref, out_ref, q_ref, near, far, kv_ref, weight_ref, part_ref, sems, sems_late,
):
    pages, _, tokens, _ = kv_ref.shape
    capacity = pages // len(masks)
    me = lax.axis_index("req")
    rows, half = out_ref.shape
    heads = q_ref.shape[0] // rows
    per_chunk = CHUNK // tokens
    pages_in = [
        pltpu.make_async_copy(
            kv_hbm.at[pl.ds((me ^ mask) * capacity, capacity)],
            kv_ref.at[pl.ds(index * capacity, capacity)],
            sems.at[1 + index],
        )
        for index, mask in enumerate(masks)
    ]
    queries_in = pltpu.make_async_copy(q_hbm, q_ref, sems.at[0])
    there = pl.ds(pl.multiple_of((1 - lax.axis_index("tp")) * half, half), half)
    late = [
        pltpu.make_async_copy(source, near.at[kind], sems_late.at[kind])
        for kind, source in enumerate((sum_hbm, total_hbm, top_hbm))
    ] + [
        pltpu.make_async_copy(weight_hbm.at[:, there], weight_ref, sems_late.at[3]),
        pltpu.make_async_copy(part_hbm, part_ref, sems_late.at[4]),
    ]
    seen = [seen_ref[(me ^ mask) * capacity + rank] for mask in masks for rank in range(capacity)]
    ahead = max(2 * per_chunk // capacity, 1)
    split = ahead * capacity
    for copy in [queries_in] + pages_in:
        copy.start()
    for copy in [queries_in] + pages_in[:ahead]:
        copy.wait()
    for copy in late:
        copy.start()

    def steps(head, begin, end, state):
        query = q_ref[head * rows : (head + 1) * rows, :]
        for start in range(begin, end, per_chunk):
            span = slice(start, min(start + per_chunk, end))
            state = page_step(query, kv_ref[span, 0], kv_ref[span, 1], seen[span], state)
        return state

    for head in range(heads):
        state = steps(head, 0, split, None)
        for kind in range(3):
            far[kind, head * rows : (head + 1) * rows, :] = state[kind]
    for copy in pages_in[ahead:] + late:
        copy.wait()
    for head in range(heads):
        here = slice(head * rows, (head + 1) * rows)
        state = steps(head, split, pages, (far[0, here, :], far[1, here, :], far[2, here, :]))
        top = jnp.maximum(near[2, here, :], state[2])
        fade_near = jnp.exp2((near[2, here, :] - top) * SCORE_SCALE)
        fade_far = jnp.exp2((state[2] - top) * SCORE_SCALE)
        summed = near[0, here, :] * fade_near + state[0] * fade_far
        total = near[1, here, :] * fade_near + state[1] * fade_far
        context_ref[:, head * HEAD_SIZE : (head + 1) * HEAD_SIZE] = (summed / total).astype(BF16)
    for start in range(0, half, 256):
        tile = slice(start, start + 256)
        out_ref[:, tile] = (
            jnp.dot(context_ref[...], weight_ref[:, tile], preferred_element_type=F32)
            + part_ref[:, tile]
        ).astype(BF16)


def attend_late(seen, queries, state, weight, part, kv, masks):
    rows, half = part.shape
    count = queries.shape[0]
    pages = len(masks) * kv.shape[0] // lax.axis_size("req")
    return pl.pallas_call(
        functools.partial(attend_late_kernel, masks),
        out_shape=(
            jax.ShapeDtypeStruct((rows, count // rows * HEAD_SIZE), BF16),
            jax.ShapeDtypeStruct((rows, half), BF16),
        ),
        in_specs=[SMEM] + [HBM] * 7,
        out_specs=(VMEM, VMEM),
        scratch_shapes=[
            pltpu.VMEM(queries.shape, BF16),
            pltpu.VMEM((3, count, HEAD_SIZE), F32),
            pltpu.VMEM((3, count, HEAD_SIZE), F32),
            pltpu.VMEM((pages,) + kv.shape[1:], BF16),
            pltpu.VMEM((weight.shape[0], half), BF16),
            pltpu.VMEM((rows, half), F32),
            pltpu.SemaphoreType.DMA((1 + len(masks),)),
            pltpu.SemaphoreType.DMA((5,)),
        ],
        compiler_params=params(60),
        cost_estimate=LIGHT,
        name="attend_late",
    )(seen, queries, *state, weight, part, kv)


def mixer_out_kernel(
    core_ref, gated_ref, scale_ref, weight_ref, attn_hbm, theirs_ref, ours_ref, attn_ref, sem
):
    half = ours_ref.shape[1]
    mine = pl.ds(pl.multiple_of(core_ref[0] * half, half), half)
    cut = pltpu.make_async_copy(attn_hbm.at[:, mine], attn_ref, sem.at[0])
    cut.start()
    for start in range(0, half, 256):
        for core, out_ref in ((1 - core_ref[0], theirs_ref), (core_ref[0], ours_ref)):
            here = pl.ds(pl.multiple_of(core * half + start, 256), 256)
            out_ref[:, start : start + 256] = (
                jnp.dot(gated_ref[...], weight_ref[:, here], preferred_element_type=F32)
                * scale_ref[...]
            )
    cut.wait()


def mixer_out(core, gated, scale, weight, attn_weight):
    rows, depth = gated.shape
    width = weight.shape[1]
    return pl.pallas_call(
        mixer_out_kernel,
        out_shape=(jax.ShapeDtypeStruct((rows, width // 2), F32),) * 2
        + (jax.ShapeDtypeStruct((attn_weight.shape[0], width // 2), BF16),),
        in_specs=[SMEM] + [VMEM] * 3 + [HBM],
        out_specs=(VMEM,) * 3,
        scratch_shapes=[pltpu.SemaphoreType.DMA((1,))],
        compiler_params=params(16),
        cost_estimate=LIGHT,
        name="mixer_out",
    )(core, gated, scale, weight, attn_weight)


def ours_kernel(context_ref, weight_ref, part_ref, out_ref):
    for start in range(0, out_ref.shape[1], 256):
        tile = slice(start, start + 256)
        out_ref[:, tile] = (
            jnp.dot(context_ref[...], weight_ref[:, tile], preferred_element_type=F32)
            + part_ref[:, tile]
        ).astype(BF16)


def ours_half(context, weight, part):
    return pl.pallas_call(
        ours_kernel,
        out_shape=jax.ShapeDtypeStruct(part.shape, BF16),
        in_specs=[VMEM] * 3,
        out_specs=VMEM,
        compiler_params=params(16),
        cost_estimate=LIGHT,
        name="ours_half",
    )(context, weight, part)


def shards(
    tokens,
    attn_gain,
    w_query,
    key_weight,
    value_weight,
    w_attn_out,
    kv_pages,
    page_table,
    cached_len,
    w_gate_z,
    w_ssm_in,
    w_bc,
    w_dt,
    conv_w_x,
    conv_w_bc,
    conv_x_state,
    conv_bc_state,
    dt_bias,
    decay_rate,
    skip_gain,
    mixer_gain,
    w_mixer_out,
    ssm_state,
):
    swap = [(0, 1), (1, 0)]
    core = lax.axis_index("tp").astype(jnp.int32).reshape(1)
    row_count = tokens.shape[0]
    devices = lax.axis_size("req")
    pages_dev = kv_pages.shape[0]
    capacity = pages_dev // devices
    page_size = kv_pages.shape[3]
    length = cached_len[0]

    want, seen = wanted(page_table, cached_len, devices, pages_dev, page_size)
    cosine, sine = rope_tables(length + jnp.arange(row_count, dtype=jnp.int32))
    other = lax.ppermute(tokens, "tp", swap)

    def exchange(blocks):
        return lax.all_to_all(blocks, "req", split_axis=0, concat_axis=0, tiled=True)

    fetched, own = gather_pages(
        exchange(want), kv_pages.reshape((pages_dev, 2, page_size, HEAD_SIZE)), capacity
    )
    arrived = exchange(fetched.reshape((devices, capacity) + fetched.shape[1:])).reshape(
        fetched.shape
    )

    heads = w_dt.shape[1]
    queries, fresh_keys, fresh_values, gated, squares, last_state = front(
        core, tokens, other, attn_gain[None, :], cosine, sine,
        conv_x_state, conv_bc_state, conv_w_x, conv_w_bc,
        dt_bias[None, :], decay_rate[None, :], skip_gain,
        mixer_gain[None, :],
        w_dt.T, w_bc, w_ssm_in, w_gate_z, w_query, key_weight, value_weight,
        ssm_state.reshape((heads * MP, MN)),
    )
    total = squares + lax.ppermute(squares, "tp", swap)
    scale = lax.rsqrt(total.reshape((row_count, 1)) / DSSM + EPSILON)
    part_theirs, part_ours, weight_ours = mixer_out(core, gated, scale, w_mixer_out, w_attn_out)
    state = attend_early(
        seen, queries, (fresh_keys, fresh_values), row_count, [own], [0], [(0, None)]
    )
    context, theirs = attend_late(
        seen, queries, state, w_attn_out, part_theirs, arrived, list(range(1, devices))
    )
    received = lax.ppermute(theirs, "tp", swap)
    ours = ours_half(context, weight_ours, part_ours)
    mixed = (ours.astype(F32) + received.astype(F32)).astype(BF16)
    return (mixed, last_state.reshape(ssm_state.shape))


def solution(mesh):
    return jax.shard_map(
        shards,
        mesh=mesh,
        in_specs=(
            P("req", "tp"),
            P(),
            P(None, "tp"),
            P(None, "tp"),
            P(None, "tp"),
            P("tp", None),
            P("req", None, "tp", None, None),
            P("req", None),
            P("req"),
            P(None, "tp"),
            P(None, "tp"),
            P(),
            P(None, "tp"),
            P(None, "tp"),
            P(),
            P("req", None, "tp"),
            P("req", None, None),
            P("tp"),
            P("tp"),
            P("tp"),
            P("tp"),
            P("tp", None),
            P("req", "tp", None, None),
        ),
        out_specs=(P("req", "tp"), P("req", "tp", None, None)),
        check_vma=False,
    )
```

```python
import functools

import jax
import jax.numpy as jnp
from jax import lax
from jax.experimental import pallas as pl
from jax.experimental.pallas import tpu as pltpu
from jax.sharding import PartitionSpec as P

HEAD_SIZE = 128
MP = 64
MN = 256
DSSM = 1536

EPSILON = 1e-05
ROPE_BASE = 100000.0
NEG_FILL = -1e30
LOG2E = 1.4426950408889634
SCORE_SCALE = HEAD_SIZE ** (-0.5) * LOG2E

VMEM = pl.BlockSpec(memory_space=pltpu.VMEM)
SMEM = pl.BlockSpec(memory_space=pltpu.SMEM)
HBM = pl.BlockSpec(memory_space=pltpu.HBM)
F32 = jnp.float32
BF16 = jnp.bfloat16
LIGHT = pl.CostEstimate(flops=10**6, bytes_accessed=10**4, transcendentals=0)


def params(mebibytes):
    return pltpu.CompilerParams(vmem_limit_bytes=mebibytes * 2**20)


def rope_tables(token_positions):
    half_width = HEAD_SIZE // 2
    inverse = ROPE_BASE ** (-2.0 * jnp.arange(half_width, dtype=F32) / HEAD_SIZE)
    angles = token_positions.astype(F32)[:, None] * inverse[None, :]
    cosine, sine = jnp.cos(angles), jnp.sin(angles)
    return (
        jnp.concatenate([cosine, cosine], axis=-1),
        jnp.concatenate([-sine, sine], axis=-1),
    )


def want_kernel(pages_dev, capacity, page_size, table_ref, length_ref, want_ref, seen_ref, slots, counts):
    for i in range(counts.shape[0]):
        counts[i] = 0
    for i in range(slots.shape[0]):
        slots[i] = 0
        seen_ref[i] = 0
    for page in range(table_ref.shape[1]):
        entry = table_ref[0, page]
        owner = entry // pages_dev
        rank = counts[owner]
        counts[owner] = rank + 1
        place = owner * capacity + rank
        slots[place] = entry - owner * pages_dev
        seen_ref[place] = jnp.clip(length_ref[0] - page * page_size, 0, page_size)
    lane = lax.broadcasted_iota(jnp.int32, want_ref.shape[1:], 1)
    for owner in range(want_ref.shape[0]):
        tile = jnp.zeros(want_ref.shape[1:], jnp.int32)
        for rank in range(capacity):
            tile = jnp.where(lane == rank, slots[owner * capacity + rank], tile)
        want_ref[owner] = tile


def wanted(table, length, devices, pages_dev, page_size):
    capacity = pages_dev // devices
    return pl.pallas_call(
        functools.partial(want_kernel, pages_dev, capacity, page_size),
        out_shape=(
            jax.ShapeDtypeStruct((devices, 1, 128), jnp.int32),
            jax.ShapeDtypeStruct((devices * capacity,), jnp.int32),
        ),
        in_specs=[SMEM, SMEM],
        out_specs=(VMEM, SMEM),
        scratch_shapes=[
            pltpu.SMEM((devices * capacity,), jnp.int32),
            pltpu.SMEM((devices,), jnp.int32),
        ],
        name="wanted",
    )(table, length)


def gather_kernel(capacity, asked_hbm, pages_ref, out_ref, own_ref, asked, held, sem, sems_in, sems_out):
    me = lax.axis_index("req")
    load = pltpu.make_async_copy(asked_hbm, asked, sem.at[0])
    load.start()
    parts = sems_in.shape[0]
    size = held.shape[0] // parts
    reads = [
        pltpu.make_async_copy(
            pages_ref.at[pl.ds(part * size, size)],
            held.at[pl.ds(part * size, size)],
            sems_in.at[part],
        )
        for part in range(parts)
    ]
    for read in reads:
        read.start()
    load.wait()
    for read in reads:
        read.wait()
    writes = []
    for index in range(out_ref.shape[0]):
        slot = asked[index // capacity, 0, index % capacity]
        writes.append(
            pltpu.make_async_copy(held.at[slot], out_ref.at[index], sems_out.at[index])
        )
    for rank in range(capacity):
        slot = asked[me, 0, rank]
        writes.append(
            pltpu.make_async_copy(
                held.at[slot], own_ref.at[rank], sems_out.at[out_ref.shape[0] + rank]
            )
        )
    for write in writes:
        write.start()
    for write in writes:
        write.wait()


def gather_pages(asked, kv_pages, capacity):
    count = asked.shape[0] * capacity
    page = kv_pages.shape[1:]
    return pl.pallas_call(
        functools.partial(gather_kernel, capacity),
        out_shape=(
            jax.ShapeDtypeStruct((count,) + page, kv_pages.dtype),
            jax.ShapeDtypeStruct((capacity,) + page, kv_pages.dtype),
        ),
        in_specs=[HBM, HBM],
        out_specs=(HBM, HBM),
        scratch_shapes=[
            pltpu.SMEM(asked.shape, jnp.int32),
            pltpu.VMEM(kv_pages.shape, kv_pages.dtype),
            pltpu.SemaphoreType.DMA((1,)),
            pltpu.SemaphoreType.DMA((4,)),
            pltpu.SemaphoreType.DMA((count + capacity,)),
        ],
        compiler_params=params(60),
        cost_estimate=LIGHT,
        name="gather_pages",
    )(asked, kv_pages)


def silu(value):
    return value / (1.0 + jnp.exp(-value))


def front_kernel(
    core_ref, mine_ref, other_ref, gain_ref, cos_ref, sin_ref,
    histx_ref, histbc_ref, convx_ref, convbc_ref, bias_ref, rate_ref, skip_ref, mixer_gain_ref,
    wdt_hbm, wbc_hbm, wx_hbm, wz_hbm, wq_hbm, wk_hbm, wv_hbm, state_hbm,
    q_ref, k_ref, v_ref, gated_ref, square_ref, last_hbm,
    normed, wdt, wbc, wx, wz, wq, wkv, state_ref, last_ref, sems,
    x_ref, z_ref, bc_ref, padded, inner, cum, cum_t, step_size, b_ref, c_ref,
):
    copies = [
        pltpu.make_async_copy(source, target, sems.at[i])
        for i, (source, target) in enumerate(
            (
                (wdt_hbm, wdt),
                (wbc_hbm, wbc),
                (wx_hbm, wx),
                (wz_hbm, wz),
                (state_hbm, state_ref),
                (wq_hbm, wq),
                (wk_hbm, wkv.at[:, 0:HEAD_SIZE]),
                (wv_hbm, wkv.at[:, HEAD_SIZE : 2 * HEAD_SIZE]),
            )
        )
    ]
    for copy in copies:
        copy.start()

    rows, half = mine_ref.shape
    core = core_ref[0]
    here = pl.ds(pl.multiple_of(core * half, half), half)
    there = pl.ds(pl.multiple_of((1 - core) * half, half), half)
    step = 64

    def norm_rows(i, carry):
        block = pl.ds(pl.multiple_of(i * step, step), step)
        mine = mine_ref[block, :].astype(F32)
        other = other_ref[block, :].astype(F32)
        total = jnp.sum(mine * mine + other * other, axis=-1, keepdims=True)
        scale = lax.rsqrt(total / (2 * half) + EPSILON)
        normed[block, here] = (mine * scale * gain_ref[:, here]).astype(BF16)
        normed[block, there] = (other * scale * gain_ref[:, there]).astype(BF16)
        return carry

    lax.fori_loop(0, rows // step, norm_rows, 0)

    def dense(weight, target):
        for start in range(0, weight.shape[1], 256):
            tile = slice(start, start + 256)
            target[:, tile] = jnp.dot(
                normed[...], weight[:, tile], preferred_element_type=F32
            ).astype(BF16)

    copies[0].wait()
    raw = lax.dot_general(
        normed[...], wdt[...], (((1,), (1,)), ((), ())), preferred_element_type=F32
    ) + bias_ref[...]
    heads = raw.shape[1]
    copies[1].wait()
    dense(wbc, bc_ref)
    copies[2].wait()
    dense(wx, x_ref)
    copies[3].wait()
    dense(wz, z_ref)

    taps = convx_ref.shape[0]
    group = 2 * MP
    middle = rows // 2

    def conv(history, fresh, kernel):
        width = fresh.shape[1]
        padded[0:8, 0:width] = jnp.zeros((8, width), F32)
        padded[8 - (taps - 1) : 8, 0:width] = history.astype(F32)
        padded[8 : 8 + rows, 0:width] = fresh.astype(F32)
        summed = padded[9 - taps : 9 - taps + rows, 0:width] * kernel[0:1, :]
        for tap in range(1, taps):
            begin = 9 - taps + tap
            summed = summed + padded[begin : begin + rows, 0:width] * kernel[tap : tap + 1, :]
        return silu(summed).astype(BF16)

    for start in range(0, 2 * MN, group):
        part = conv(
            histbc_ref[0, :, start : start + group],
            bc_ref[:, start : start + group],
            convbc_ref[:, start : start + group],
        )
        if start < MN:
            b_ref[:, start : start + group] = part
        else:
            c_ref[:, start - MN : start - MN + group] = part

    size = jnp.maximum(raw, 0.0) + jnp.log1p(jnp.exp(-jnp.abs(raw)))
    step_size[:, 0:heads] = size
    row_index = lax.broadcasted_iota(jnp.int32, (rows, rows), 0)
    column_index = lax.broadcasted_iota(jnp.int32, (rows, rows), 1)
    causal = column_index <= row_index
    cum[...] = jnp.zeros((rows, 128), F32)
    cum[:, 0:heads] = -size * (rate_ref[...] * LOG2E)
    cum[...] = jnp.dot(
        causal.astype(F32), cum[...], precision=lax.Precision.HIGHEST, preferred_element_type=F32
    )
    cum_t[...] = cum[...].T
    inner[...] = jnp.where(
        causal,
        lax.dot_general(c_ref[...], b_ref[...], CONTRACT_LAST, preferred_element_type=F32),
        0.0,
    )
    copies[4].wait()
    first = lax.broadcasted_iota(jnp.int32, (1, group), 1) < MP
    first_rows = lax.broadcasted_iota(jnp.int32, (group, 1), 0) < MP
    squares = jnp.zeros((rows, group), F32)
    for pair in range(heads // 2):
        cols = slice(pair * group, (pair + 1) * group)
        one, two = 2 * pair, 2 * pair + 1
        x_rows = conv(histx_ref[0, :, cols], x_ref[:, cols], convx_ref[:, cols]).astype(F32)
        sizes = jnp.where(first, step_size[:, one : one + 1], step_size[:, two : two + 1])
        fades = jnp.where(first, cum[:, one : one + 1], cum[:, two : two + 1])
        last_fade = fades[rows - 1 : rows, :]
        moved_float = x_rows * sizes
        moved = moved_float.astype(BF16)
        tail_moved = moved_float * jnp.exp2(last_fade - fades)
        state = state_ref[cols, :]
        state_high = state.astype(BF16)
        state_low = (state - state_high.astype(F32)).astype(BF16)
        carried = lax.dot_general(
            c_ref[...], state_high, CONTRACT_LAST, preferred_element_type=F32
        ) + lax.dot_general(c_ref[...], state_low, CONTRACT_LAST, preferred_element_type=F32)
        blocks = []
        for begin in (0, middle):
            end = begin + middle
            sides = []
            for head in (one, two):
                gap = cum[begin:end, head : head + 1] - cum_t[head : head + 1, 0:end]
                mixing = (jnp.exp2(jnp.minimum(gap, 0.0)) * inner[begin:end, 0:end]).astype(BF16)
                sides.append(jnp.dot(mixing, moved[0:end, :], preferred_element_type=F32))
            blocks.append(jnp.where(first, sides[0], sides[1]))
        ssm_y = (
            jnp.concatenate(blocks, axis=0)
            + carried * jnp.exp2(fades)
            + jnp.where(first, skip_ref[one], skip_ref[two]) * x_rows
        )
        gated = ssm_y * silu(z_ref[:, cols].astype(F32))
        squares = squares + gated * gated
        gated_ref[:, cols] = (gated * mixer_gain_ref[:, cols]).astype(BF16)
        added = jnp.dot(tail_moved.T.astype(BF16), b_ref[...], preferred_element_type=F32)
        ends = jnp.exp2(cum_t[one : two + 1, rows - 1 : rows])
        keep = jnp.where(first_rows, ends[0:1, :], ends[1:2, :])
        last_ref[cols, :] = keep * state + added
    square_ref[...] = jnp.sum(squares.T, axis=0, keepdims=True)
    give_back = pltpu.make_async_copy(last_ref, last_hbm, sems.at[8])
    give_back.start()

    def rope(vectors):
        return vectors * cos_ref[...] + pltpu.roll(vectors, HEAD_SIZE // 2, 1) * sin_ref[...]

    copies[5].wait()
    for tile in range(wq.shape[1] // 256):
        two_heads = jnp.dot(
            normed[...], wq[:, tile * 256 : tile * 256 + 256], preferred_element_type=F32
        )
        for side in range(2):
            head = 2 * tile + side
            q_ref[head * rows : (head + 1) * rows, :] = rope(
                two_heads[:, side * HEAD_SIZE : (side + 1) * HEAD_SIZE]
            ).astype(BF16)
    copies[6].wait()
    copies[7].wait()
    key_value = jnp.dot(normed[...], wkv[...], preferred_element_type=F32)
    k_ref[...] = rope(key_value[:, :HEAD_SIZE]).astype(BF16)
    v_ref[...] = key_value[:, HEAD_SIZE:].astype(BF16)
    give_back.wait()


def front(
    core, mine, other, gain, cosine, sine,
    histx, histbc, convx, convbc, bias, rate, skip, mixer_gain,
    wdt, wbc, wx, wz, wq, wk, wv, state,
):
    rows, half = mine.shape
    width = 2 * half

    def out(shape, dtype=BF16):
        return jax.ShapeDtypeStruct(shape, dtype)

    return pl.pallas_call(
        front_kernel,
        out_shape=(
            out((wq.shape[1] // HEAD_SIZE * rows, HEAD_SIZE)),
            out((rows, wk.shape[1])),
            out((rows, wv.shape[1])),
            out((rows, wx.shape[1])),
            out((1, rows), F32),
            out(state.shape, F32),
        ),
        in_specs=[SMEM] + [VMEM] * 11 + [SMEM, VMEM] + [HBM] * 8,
        out_specs=(VMEM,) * 5 + (HBM,),
        scratch_shapes=[
            pltpu.VMEM((rows, width), BF16),
            pltpu.VMEM(wdt.shape, BF16),
            pltpu.VMEM(wbc.shape, BF16),
            pltpu.VMEM(wx.shape, BF16),
            pltpu.VMEM(wz.shape, BF16),
            pltpu.VMEM(wq.shape, BF16),
            pltpu.VMEM((width, 2 * HEAD_SIZE), BF16),
            pltpu.VMEM(state.shape, F32),
            pltpu.VMEM(state.shape, F32),
            pltpu.SemaphoreType.DMA((9,)),
            pltpu.VMEM((rows, wx.shape[1]), BF16),
            pltpu.VMEM((rows, wz.shape[1]), BF16),
            pltpu.VMEM((rows, wbc.shape[1]), BF16),
            pltpu.VMEM((rows + 8, 2 * MP), F32),
            pltpu.VMEM((rows, rows), F32),
            pltpu.VMEM((rows, 128), F32),
            pltpu.VMEM((128, rows), F32),
            pltpu.VMEM((rows, 128), F32),
            pltpu.VMEM((rows, MN), BF16),
            pltpu.VMEM((rows, MN), BF16),
        ],
        compiler_params=params(60),
        cost_estimate=LIGHT,
        name="front",
    )(
        core, mine, other, gain, cosine, sine,
        histx, histbc, convx, convbc, bias, rate, skip, mixer_gain,
        wdt, wbc, wx, wz, wq, wk, wv, state,
    )


CONTRACT_LAST = (((1,), (1,)), ((), ()))
CHUNK = 512


def across(column, width):
    return jnp.concatenate([column] * (width // HEAD_SIZE), axis=1)


def softmax_step(scores, values, state):
    count = scores.shape[1]
    top = jnp.broadcast_to(jnp.max(scores, axis=-1, keepdims=True), (scores.shape[0], HEAD_SIZE))
    if state is not None:
        top = jnp.maximum(state[2], top)
    weights = jnp.exp2((scores - across(top, count)) * SCORE_SCALE).astype(BF16)
    values = jnp.concatenate([values, jnp.ones((count, HEAD_SIZE), BF16)], axis=1)
    added = jnp.dot(weights, values, preferred_element_type=F32)
    summed, total = added[:, :HEAD_SIZE], added[:, HEAD_SIZE:]
    if state is not None:
        fade = jnp.exp2((state[2] - top) * SCORE_SCALE)
        summed, total = state[0] * fade + summed, state[1] * fade + total
    return summed, total, top


def page_step(query, keys, values, seen, state):
    pages, tokens, width = keys.shape
    scores = lax.dot_general(
        query, keys.reshape(pages * tokens, width), CONTRACT_LAST, preferred_element_type=F32
    )
    token = lax.broadcasted_iota(jnp.int32, (1, tokens), 1)
    hide = jnp.concatenate(
        [jnp.where(token >= seen[page], NEG_FILL, 0.0) for page in range(pages)], axis=1
    )
    return softmax_step(scores + hide, values.reshape(pages * tokens, width), state)


def attend_early_kernel(masks, picks, fresh, seen_ref, q_hbm, *refs):
    count = max(array for array, _ in picks) + 1
    given = 2 if fresh else 3
    start_hbm, arrays = refs[:given], refs[given : given + count]
    outs = refs[given + count : given + count + 3]
    q_ref, k_ref, v_ref, kv_ref, states, sems, sems_out = refs[given + count + 3 :]
    rows = k_ref.shape[0]
    pages, _, tokens, _ = kv_ref.shape
    capacity = pages // len(masks)
    me = lax.axis_index("req")
    targets = (k_ref, v_ref) if fresh else (states.at[0], states.at[1], states.at[2])
    copies = [pltpu.make_async_copy(q_hbm, q_ref, sems.at[0])]
    for index, (source, target) in enumerate(zip(start_hbm, targets)):
        copies.append(pltpu.make_async_copy(source, target, sems.at[1 + index]))
    for index, (array, entry) in enumerate(picks):
        source = arrays[array] if entry is None else arrays[array].at[entry]
        copies.append(
            pltpu.make_async_copy(
                source, kv_ref.at[pl.ds(index * capacity, capacity)], sems.at[4 + index]
            )
        )
    for copy in copies:
        copy.start()
    seen = [seen_ref[(me ^ mask) * capacity + rank] for mask in masks for rank in range(capacity)]
    row = lax.broadcasted_iota(jnp.int32, (rows, rows), 0)
    column = lax.broadcasted_iota(jnp.int32, (rows, rows), 1)
    for copy in copies:
        copy.wait()
    per_chunk = CHUNK // tokens
    sends = []
    for head, start in enumerate(range(0, q_ref.shape[0], rows)):
        here = slice(start, start + rows)
        if fresh:
            scores = lax.dot_general(
                q_ref[here, :], k_ref[...], CONTRACT_LAST, preferred_element_type=F32
            )
            state = softmax_step(jnp.where(column <= row, scores, NEG_FILL), v_ref[...], None)
        else:
            state = (states[0, here, :], states[1, here, :], states[2, here, :])
        for begin in range(0, pages, per_chunk):
            span = slice(begin, begin + per_chunk)
            state = page_step(q_ref[here, :], kv_ref[span, 0], kv_ref[span, 1], seen[span], state)
        for kind in range(3):
            states[kind, here, :] = state[kind]
            send = pltpu.make_async_copy(
                states.at[kind, here, :], outs[kind].at[here, :], sems_out.at[3 * head + kind]
            )
            send.start()
            sends.append(send)
    for send in sends:
        send.wait()


def attend_early(seen, queries, start, rows, arrays, masks, picks):
    count = queries.shape[0]
    block = arrays[0].shape[-4:]
    pages = len(masks) * block[0]
    fresh = len(start) == 2
    return pl.pallas_call(
        functools.partial(attend_early_kernel, masks, picks, fresh),
        out_shape=(jax.ShapeDtypeStruct((count, HEAD_SIZE), F32),) * 3,
        in_specs=[SMEM] + [HBM] * (1 + len(start) + len(arrays)),
        out_specs=(HBM,) * 3,
        scratch_shapes=[
            pltpu.VMEM(queries.shape, BF16),
            pltpu.VMEM((rows, HEAD_SIZE), BF16),
            pltpu.VMEM((rows, HEAD_SIZE), BF16),
            pltpu.VMEM((pages,) + block[1:], BF16),
            pltpu.VMEM((3, count, HEAD_SIZE), F32),
            pltpu.SemaphoreType.DMA((4 + len(masks),)),
            pltpu.SemaphoreType.DMA((3 * count // rows,)),
        ],
        compiler_params=params(60),
        cost_estimate=LIGHT,
        name="attend_first" if fresh else "attend_more",
    )(seen, queries, *start, *arrays)


def attend_late_kernel(
    masks, seen_ref, q_hbm, sum_hbm, total_hbm, top_hbm, weight_hbm, part_hbm, kv_hbm,
    context_ref, out_ref, q_ref, near, far, kv_ref, weight_ref, part_ref, sems, sems_late,
):
    pages, _, tokens, _ = kv_ref.shape
    capacity = pages // len(masks)
    me = lax.axis_index("req")
    rows, half = out_ref.shape
    heads = q_ref.shape[0] // rows
    per_chunk = CHUNK // tokens
    pages_in = [
        pltpu.make_async_copy(
            kv_hbm.at[pl.ds((me ^ mask) * capacity, capacity)],
            kv_ref.at[pl.ds(index * capacity, capacity)],
            sems.at[1 + index],
        )
        for index, mask in enumerate(masks)
    ]
    queries_in = pltpu.make_async_copy(q_hbm, q_ref, sems.at[0])
    there = pl.ds(pl.multiple_of((1 - lax.axis_index("tp")) * half, half), half)
    late = [
        pltpu.make_async_copy(source, near.at[kind], sems_late.at[kind])
        for kind, source in enumerate((sum_hbm, total_hbm, top_hbm))
    ] + [
        pltpu.make_async_copy(weight_hbm.at[:, there], weight_ref, sems_late.at[3]),
        pltpu.make_async_copy(part_hbm, part_ref, sems_late.at[4]),
    ]
    seen = [seen_ref[(me ^ mask) * capacity + rank] for mask in masks for rank in range(capacity)]
    ahead = max(2 * per_chunk // capacity, 1)
    split = ahead * capacity
    for copy in [queries_in] + pages_in:
        copy.start()
    for copy in [queries_in] + pages_in[:ahead]:
        copy.wait()
    for copy in late:
        copy.start()

    def steps(head, begin, end, state):
        query = q_ref[head * rows : (head + 1) * rows, :]
        for start in range(begin, end, per_chunk):
            span = slice(start, min(start + per_chunk, end))
            state = page_step(query, kv_ref[span, 0], kv_ref[span, 1], seen[span], state)
        return state

    for head in range(heads):
        state = steps(head, 0, split, None)
        for kind in range(3):
            far[kind, head * rows : (head + 1) * rows, :] = state[kind]
    for copy in pages_in[ahead:] + late:
        copy.wait()
    for head in range(heads):
        here = slice(head * rows, (head + 1) * rows)
        state = steps(head, split, pages, (far[0, here, :], far[1, here, :], far[2, here, :]))
        top = jnp.maximum(near[2, here, :], state[2])
        fade_near = jnp.exp2((near[2, here, :] - top) * SCORE_SCALE)
        fade_far = jnp.exp2((state[2] - top) * SCORE_SCALE)
        summed = near[0, here, :] * fade_near + state[0] * fade_far
        total = near[1, here, :] * fade_near + state[1] * fade_far
        context_ref[:, head * HEAD_SIZE : (head + 1) * HEAD_SIZE] = (summed / total).astype(BF16)
    for start in range(0, half, 256):
        tile = slice(start, start + 256)
        out_ref[:, tile] = (
            jnp.dot(context_ref[...], weight_ref[:, tile], preferred_element_type=F32)
            + part_ref[:, tile]
        ).astype(BF16)


def attend_late(seen, queries, state, weight, part, kv, masks):
    rows, half = part.shape
    count = queries.shape[0]
    pages = len(masks) * kv.shape[0] // lax.axis_size("req")
    return pl.pallas_call(
        functools.partial(attend_late_kernel, masks),
        out_shape=(
            jax.ShapeDtypeStruct((rows, count // rows * HEAD_SIZE), BF16),
            jax.ShapeDtypeStruct((rows, half), BF16),
        ),
        in_specs=[SMEM] + [HBM] * 7,
        out_specs=(VMEM, VMEM),
        scratch_shapes=[
            pltpu.VMEM(queries.shape, BF16),
            pltpu.VMEM((3, count, HEAD_SIZE), F32),
            pltpu.VMEM((3, count, HEAD_SIZE), F32),
            pltpu.VMEM((pages,) + kv.shape[1:], BF16),
            pltpu.VMEM((weight.shape[0], half), BF16),
            pltpu.VMEM((rows, half), F32),
            pltpu.SemaphoreType.DMA((1 + len(masks),)),
            pltpu.SemaphoreType.DMA((5,)),
        ],
        compiler_params=params(60),
        cost_estimate=LIGHT,
        name="attend_late",
    )(seen, queries, *state, weight, part, kv)


def mixer_out_kernel(
    core_ref, gated_ref, scale_ref, weight_ref, attn_hbm, theirs_ref, ours_ref, attn_ref, sem
):
    half = ours_ref.shape[1]
    mine = pl.ds(pl.multiple_of(core_ref[0] * half, half), half)
    cut = pltpu.make_async_copy(attn_hbm.at[:, mine], attn_ref, sem.at[0])
    cut.start()
    for start in range(0, half, 256):
        for core, out_ref in ((1 - core_ref[0], theirs_ref), (core_ref[0], ours_ref)):
            here = pl.ds(pl.multiple_of(core * half + start, 256), 256)
            out_ref[:, start : start + 256] = (
                jnp.dot(gated_ref[...], weight_ref[:, here], preferred_element_type=F32)
                * scale_ref[...]
            )
    cut.wait()


def mixer_out(core, gated, scale, weight, attn_weight):
    rows, depth = gated.shape
    width = weight.shape[1]
    return pl.pallas_call(
        mixer_out_kernel,
        out_shape=(jax.ShapeDtypeStruct((rows, width // 2), F32),) * 2
        + (jax.ShapeDtypeStruct((attn_weight.shape[0], width // 2), BF16),),
        in_specs=[SMEM] + [VMEM] * 3 + [HBM],
        out_specs=(VMEM,) * 3,
        scratch_shapes=[pltpu.SemaphoreType.DMA((1,))],
        compiler_params=params(16),
        cost_estimate=LIGHT,
        name="mixer_out",
    )(core, gated, scale, weight, attn_weight)


def ours_kernel(context_ref, weight_ref, part_ref, out_ref):
    for start in range(0, out_ref.shape[1], 256):
        tile = slice(start, start + 256)
        out_ref[:, tile] = (
            jnp.dot(context_ref[...], weight_ref[:, tile], preferred_element_type=F32)
            + part_ref[:, tile]
        ).astype(BF16)


def ours_half(context, weight, part):
    return pl.pallas_call(
        ours_kernel,
        out_shape=jax.ShapeDtypeStruct(part.shape, BF16),
        in_specs=[VMEM] * 3,
        out_specs=VMEM,
        compiler_params=params(16),
        cost_estimate=LIGHT,
        name="ours_half",
    )(context, weight, part)


def shards(
    tokens,
    attn_gain,
    w_query,
    key_weight,
    value_weight,
    w_attn_out,
    kv_pages,
    page_table,
    cached_len,
    w_gate_z,
    w_ssm_in,
    w_bc,
    w_dt,
    conv_w_x,
    conv_w_bc,
    conv_x_state,
    conv_bc_state,
    dt_bias,
    decay_rate,
    skip_gain,
    mixer_gain,
    w_mixer_out,
    ssm_state,
):
    swap = [(0, 1), (1, 0)]
    core = lax.axis_index("tp").astype(jnp.int32).reshape(1)
    row_count = tokens.shape[0]
    devices = lax.axis_size("req")
    pages_dev = kv_pages.shape[0]
    capacity = pages_dev // devices
    page_size = kv_pages.shape[3]
    length = cached_len[0]

    want, seen = wanted(page_table, cached_len, devices, pages_dev, page_size)
    cosine, sine = rope_tables(length + jnp.arange(row_count, dtype=jnp.int32))
    other = lax.ppermute(tokens, "tp", swap)

    def exchange(blocks):
        return lax.all_to_all(blocks, "req", split_axis=0, concat_axis=0, tiled=True)

    fetched, own = gather_pages(
        exchange(want), kv_pages.reshape((pages_dev, 2, page_size, HEAD_SIZE)), capacity
    )
    arrived = exchange(fetched.reshape((devices, capacity) + fetched.shape[1:])).reshape(
        fetched.shape
    )

    heads = w_dt.shape[1]
    queries, fresh_keys, fresh_values, gated, squares, last_state = front(
        core, tokens, other, attn_gain[None, :], cosine, sine,
        conv_x_state, conv_bc_state, conv_w_x, conv_w_bc,
        dt_bias[None, :], decay_rate[None, :], skip_gain,
        mixer_gain[None, :],
        w_dt.T, w_bc, w_ssm_in, w_gate_z, w_query, key_weight, value_weight,
        ssm_state.reshape((heads * MP, MN)),
    )
    total = squares + lax.ppermute(squares, "tp", swap)
    scale = lax.rsqrt(total.reshape((row_count, 1)) / DSSM + EPSILON)
    part_theirs, part_ours, weight_ours = mixer_out(core, gated, scale, w_mixer_out, w_attn_out)
    state = attend_early(
        seen, queries, (fresh_keys, fresh_values), row_count, [own], [0], [(0, None)]
    )
    context, theirs = attend_late(
        seen, queries, state, w_attn_out, part_theirs, arrived, list(range(1, devices))
    )
    received = lax.ppermute(theirs, "tp", swap)
    ours = ours_half(context, weight_ours, part_ours)
    mixed = (ours.astype(F32) + received.astype(F32)).astype(BF16)
    return (mixed, last_state.reshape(ssm_state.shape))


def solution(mesh):
    return jax.shard_map(
        shards,
        mesh=mesh,
        in_specs=(
            P("req", "tp"),
            P(),
            P(None, "tp"),
            P(None, "tp"),
            P(None, "tp"),
            P("tp", None),
            P("req", None, "tp", None, None),
            P("req", None),
            P("req"),
            P(None, "tp"),
            P(None, "tp"),
            P(),
            P(None, "tp"),
            P(None, "tp"),
            P(),
            P("req", None, "tp"),
            P("req", None, None),
            P("tp"),
            P("tp"),
            P("tp"),
            P("tp"),
            P("tp", None),
            P("req", "tp", None, None),
        ),
        out_specs=(P("req", "tp"), P("req", "tp", None, None)),
        check_vma=False,
    )
```
